512 devices in a mesh: hist: 128 (over z, x, core), mp: 4 (over y).
Axes of the slice: x: 4, y: 4, z: 16, core: 2. Of those that a mesh axis runs over, the one named last changes fastest.
Arguments:
- candidates: bfloat16 [1024, 1024], P('hist'), may hold values from -6 to 6
- actions: bfloat16 [256, 1024], P('hist'), may hold values from -6 to 6
- hist_keys: bfloat16 [131072, 1024], P('hist', 'mp'), may hold values from -6 to 6
- hist_values: bfloat16 [131072, 1024], P('hist', 'mp'), may hold values from -6 to 6
- w_query: bfloat16 [1024, 1024], P(None, 'mp'), may hold values from -0.1875 to 0.1875
- w_gate: bfloat16 [1024, 1024], P(None, 'mp'), may hold values from -0.1875 to 0.1875
- w_key: bfloat16 [1024, 1024], P(None, 'mp'), may hold values from -0.1875 to 0.1875
- w_value: bfloat16 [1024, 1024], P(None, 'mp'), may hold values from -0.1875 to 0.1875
- w_out: bfloat16 [1024, 1024], P('mp'), may hold values from -0.1875 to 0.1875
- segment_list: int32 [4, 128], replicated, may hold values from -1 to 255, as said below
- segment_count: int32 [4], replicated, may hold values from 1 to 128, as said below
- segment_length: int32 [256], replicated, may hold values from 128 to 448
- new_count: int32 [4], replicated, may hold values from 1 to 64
- batch_user: int32 [128], replicated, may hold values from 0 to 3
Outputs:
- ranked: bfloat16 [1024, 1024], P('hist', 'mp')
- new_keys: bfloat16 [131072, 1024], P('hist', 'mp')
- new_values: bfloat16 [131072, 1024], P('hist', 'mp')
The draws below stay inside these ranges and needn't reach their ends.
Inputs may be any that keep to these rules, and one draw needn't show every extreme that they name: `segment_list`: row u lists (segment_count)[u] distinct segment ids and then -1; every id of 0 to 255 is listed by exactly one user; the last listed segment of a user receives its new actions. `segment_count`: the counts sum to 256; one user lists exactly 128 segments.
All inputs are finite; a program needn't handle non-finite values.
Results may differ from the reference program's by a relative error of at most 0.0045.
Values may be sent and summed in bfloat16 or wider, within the bound.
No kernel may reach another device: no remote copies, remote signals or barrier semaphores. Data moves between devices by JAX's collectives and lax.ppermute only.
A program may use at most 64 MiB of HBM per device.

```python
import math
import jax
import jax.numpy as jnp
from jax import lax

D = 1024
H = 8
DH = 128
SEG = 512
NEW = 64
SEG_DEV = 2
MB = 8
USERS = 4
TOTAL_SEGS = 256
MOSTSEG = 128
ROWS = 131072
CANDS = 1024
ACT_DEV = 2
N_HIST = 128


def user_segments(key):
    key_big, key_cuts, key_perm = jax.random.split(key, 3)
    biggest = jax.random.randint(key_big, (), 0, USERS)
    spare = TOTAL_SEGS - MOSTSEG - (USERS - 1)
    cut_points = jnp.sort(jax.random.randint(key_cuts, (USERS - 2,), 0, spare + 1))
    edges = jnp.concatenate([jnp.zeros((1,), jnp.int32), cut_points.astype(jnp.int32), jnp.full((1,), spare, jnp.int32)])
    others = edges[1:] - edges[:-1] + 1
    user_ids = jnp.arange(USERS, dtype=jnp.int32)
    other_index = jnp.clip(user_ids - (user_ids > biggest).astype(jnp.int32), 0, USERS - 2)
    counts = jnp.where(user_ids == biggest, MOSTSEG, others[other_index]).astype(jnp.int32)
    first_device = user_ids * NEW // ACT_DEV
    open_device = jnp.where(user_ids == 1, first_device + N_HIST // 2, first_device + 1) % N_HIST
    open_ids = (open_device * SEG_DEV).astype(jnp.int32)
    shuffled = jax.random.permutation(key_perm, TOTAL_SEGS).astype(jnp.int32)
    is_open = jnp.any(shuffled[:, None] == open_ids[None, :], axis=1).astype(jnp.int32)
    scores = is_open * TOTAL_SEGS + jnp.arange(TOTAL_SEGS, dtype=jnp.int32)
    rest = shuffled[jnp.argsort(scores)]
    older = counts - 1
    offsets = jnp.cumsum(older) - older
    slot_ids = jnp.arange(MOSTSEG, dtype=jnp.int32)
    spots = jnp.clip(offsets[:, None] + slot_ids[None, :], 0, TOTAL_SEGS - 1)
    listing = jnp.where(slot_ids[None, :] < older[:, None], rest[spots], jnp.where(slot_ids[None, :] == older[:, None], open_ids[:, None], -1)).astype(jnp.int32)
    return (counts, listing)


def draw_segment_list(key, part):
    return user_segments(key)[1]


def draw_segment_count(key, part):
    return user_segments(key)[0]


def plant(result, own_key, low, top_value):
    spot = [jax.random.randint(jax.random.fold_in(own_key, axis), (), 0, length) for axis, length in enumerate(result.shape)]
    main_axis = result.shape.index(max(result.shape))
    beside = spot[:main_axis] + [(spot[main_axis] + 1) % result.shape[main_axis]] + spot[main_axis + 1:]
    return result.at[tuple(spot)].set(low).at[tuple(beside)].set(top_value)


def levels(stream_key, extent, shards, low, high):
    loudness, own = 1.0, jax.random.fold_in(stream_key, 6)
    for dim, blocks in shards:
        draws = jnp.exp(jax.random.uniform(jax.random.fold_in(own, dim), (blocks,), jnp.float32, low / len(shards), high / len(shards)))
        loudness = loudness * jnp.repeat(draws, extent[dim] // blocks).reshape([-1 if axis == dim else 1 for axis in range(len(extent))])
    return loudness


def gaussian(key, shape, width, most, cuts=(), held_as=jnp.bfloat16):
    gain = levels(key, shape, cuts, -0.22, 0.18) if cuts else 1.0
    entries = jax.random.normal(key, shape, jnp.float32) * width * gain
    return jnp.minimum(jnp.maximum(entries, -most), most).astype(held_as)


def setup_inputs(seed: int = 0) -> dict:
    key_list = jax.random.split(jax.random.key(seed), 15)
    return {
        "candidates": gaussian(key_list[0], (CANDS, D), 1.0, 6.0, ((0, 128),)),
        "actions": gaussian(key_list[1], (USERS * NEW, D), 1.0, 6.0, ((0, 128),)),
        "hist_keys": gaussian(key_list[2], (ROWS, D), 1.0, 6.0, ((0, 128), (1, 4))),
        "hist_values": gaussian(key_list[3], (ROWS, D), 1.0, 6.0, ((0, 128), (1, 4))),
        "w_query": gaussian(key_list[4], (D, D), D ** -0.5, 0.1875, ((1, 4),)),
        "w_gate": gaussian(key_list[5], (D, D), D ** -0.5, 0.1875, ((1, 4),)),
        "w_key": gaussian(key_list[6], (D, D), D ** -0.5, 0.1875, ((1, 4),)),
        "w_value": gaussian(key_list[7], (D, D), D ** -0.5, 0.1875, ((1, 4),)),
        "w_out": gaussian(key_list[8], (D, D), D ** -0.5, 0.1875, ((0, 4),)),
        "segment_list": draw_segment_list(jax.random.fold_in(key_list[14], 71), 0),
        "segment_count": draw_segment_count(jax.random.fold_in(key_list[14], 71), 0),
        "segment_length": plant(jax.random.randint(key_list[11], (TOTAL_SEGS,), SEG // 4, SEG - NEW + 1), jax.random.fold_in(key_list[11], 1), SEG // 4, SEG - NEW).astype(jnp.int32),
        "new_count": plant(jax.random.randint(key_list[12], (USERS,), 1, NEW + 1), jax.random.fold_in(key_list[12], 1), 1, NEW).astype(jnp.int32),
        "batch_user": plant(jax.random.randint(key_list[13], (N_HIST,), 0, USERS), jax.random.fold_in(key_list[13], 1), 0, USERS - 1).astype(jnp.int32),
    }


def reference(candidates, actions, hist_keys, hist_values, w_query, w_gate, w_key, w_value, w_out, segment_list, segment_count, segment_length, new_count, batch_user):
    fresh_keys = jnp.dot(actions, w_key, preferred_element_type=jnp.float32).astype(jnp.bfloat16)
    fresh_values = jnp.dot(actions, w_value, preferred_element_type=jnp.float32).astype(jnp.bfloat16)
    last_segment = jnp.take_along_axis(segment_list, (segment_count - 1)[:, None].astype(jnp.int32), axis=1)[:, 0]
    step_ids = jnp.arange(NEW, dtype=jnp.int32)
    open_length = segment_length[last_segment]
    target_row = last_segment[:, None] * SEG + open_length[:, None] + step_ids[None, :]
    target_row = jnp.where(step_ids[None, :] < new_count[:, None], target_row, TOTAL_SEGS * SEG).reshape(-1).astype(jnp.int32)
    new_keys = hist_keys.at[target_row].set(fresh_keys, mode='drop')
    new_values = hist_values.at[target_row].set(fresh_values, mode='drop')
    is_open = jnp.arange(TOTAL_SEGS, dtype=jnp.int32)[None, :] == last_segment[:, None]
    live_length = segment_length + lax.optimization_barrier(jnp.sum(jnp.where(is_open, new_count[:, None], 0), axis=0)).astype(jnp.int32)
    key_table = new_keys.reshape(TOTAL_SEGS, SEG, H, DH)
    value_table = new_values.reshape(TOTAL_SEGS, SEG, H, DH)
    queries = jnp.dot(candidates, w_query, preferred_element_type=jnp.float32).astype(jnp.bfloat16)
    gate_values = jax.nn.silu(jnp.dot(candidates, w_gate, preferred_element_type=jnp.float32))
    list_block = math.gcd(MOSTSEG, 16)
    list_steps = MOSTSEG // list_block
    positions = jnp.arange(SEG, dtype=jnp.int32)
    logit_scale = 1.0 / math.sqrt(DH)

    def per_batch(batch_index):
        user = batch_user[batch_index]
        listed = segment_list[user]
        query_matrix = lax.dynamic_slice_in_dim(queries, batch_index * MB, MB, 0).astype(jnp.float32).reshape(MB, H, DH)

        def per_block(grand_total, block_ids):
            present = block_ids >= 0
            safe_ids = jnp.maximum(block_ids, 0)
            key_block_rows = key_table[safe_ids].astype(jnp.float32).reshape(list_block * SEG, H, DH)
            value_block_rows = value_table[safe_ids].astype(jnp.float32).reshape(list_block * SEG, H, DH)
            limit = jnp.where(present, live_length[safe_ids], 0)
            row_valid = (positions[None, :] < limit[:, None]).reshape(-1).astype(jnp.float32)
            attention_logits = jnp.einsum('zoq,eoq->oze', query_matrix, key_block_rows) * logit_scale
            attention_weight = (jax.nn.silu(attention_logits) * row_valid[None, None, :]).astype(jnp.bfloat16)
            attention_weight = lax.optimization_barrier(attention_weight).astype(jnp.float32)
            return (grand_total + jnp.einsum('lne,eli->nli', attention_weight, value_block_rows), None)
        start_total = jnp.zeros((MB, H, DH), jnp.float32)
        grand_total, _ = lax.scan(per_block, start_total, listed.reshape(list_steps, list_block))
        return grand_total.reshape(MB, H * DH)
    attention = lax.map(per_batch, jnp.arange(N_HIST, dtype=jnp.int32)).reshape(N_HIST * MB, H * DH)
    row_mean = lax.optimization_barrier(jnp.mean(attention, axis=1, keepdims=True))
    centered = attention - row_mean
    variance = lax.optimization_barrier(jnp.mean(centered * centered, axis=1, keepdims=True))
    mixed_rows = (centered * lax.rsqrt(variance + 1e-05) * gate_values).astype(jnp.bfloat16)
    ranked = (candidates.astype(jnp.float32) + jnp.dot(mixed_rows, w_out, preferred_element_type=jnp.float32)).astype(jnp.bfloat16)
    return (ranked, new_keys, new_values)
```

```python
import functools
import math

import jax
import jax.numpy as jnp
from jax import lax
from jax.experimental import pallas as pl
from jax.experimental.pallas import tpu as pltpu
from jax.sharding import Mesh
from jax.sharding import PartitionSpec as P

D = 1024
DH = 128
SEG = 512
NEW = 64
USERS = 4
NZ = 16
NX = 4
NC = 2
XC = NX * NC
MP = 4
MB = 8
SEG_DEV = 2
W = D // MP
HEADS = W // DH
ZROWS = NZ * MB
FRESH = 16
PAY = ZROWS + SEG_DEV * FRESH
SCALE = 1.0 / math.sqrt(DH)
LOG2E = 1.4426950408889634
BF = jnp.bfloat16
F32 = jnp.float32

VMEM = pltpu.VMEM
SMEM = pltpu.SMEM


def vspec():
    return pl.BlockSpec(memory_space=VMEM)


def sspec():
    return pl.BlockSpec(memory_space=SMEM)


def project_kernel(cand, act, wq, wk, wv, out, rows):
    rows[...] = jnp.zeros_like(rows)
    rows[0:8] = jnp.dot(cand[...], wq[...], preferred_element_type=F32)
    rows[8:10] = jnp.dot(act[...], wk[...], preferred_element_type=F32)
    rows[10:12] = jnp.dot(act[...], wv[...], preferred_element_type=F32)
    msg = rows[...].astype(BF)
    for i in range(NZ):
        out[i] = msg


def project(cand, act, wq, wk, wv):
    return pl.pallas_call(
        project_kernel,
        out_shape=jax.ShapeDtypeStruct((NZ, 16, W), BF),
        in_specs=[vspec()] * 5,
        out_specs=vspec(),
        scratch_shapes=[pltpu.VMEM((16, W), F32)],
        name="project",
    )(cand, act, wq, wk, wv)


def spread_kernel(col, arr, out):
    x = arr[...].astype(F32)
    q = x[:, 0:8].reshape(ZROWS, W).astype(BF)
    f = x[:, 8:16].reshape(ZROWS, W).astype(BF)
    lane = lax.broadcasted_iota(jnp.int32, (XC * SEG_DEV * FRESH, ZROWS), 1)
    hot = (lane == col[...]).astype(F32).astype(BF)
    sel = jnp.dot(hot, f, preferred_element_type=F32).astype(BF)
    for t in range(XC):
        out[t, 0:ZROWS] = q
        out[t, ZROWS:PAY] = sel[t * 32 : t * 32 + 32]


def spread(col, arr):
    return pl.pallas_call(
        spread_kernel,
        out_shape=jax.ShapeDtypeStruct((XC, PAY, W), BF),
        in_specs=[vspec()] * 2,
        out_specs=vspec(),
        name="spread",
    )(col, arr)


def attend_kernel(info, maskrow, arr, keys, vals, part, new_keys, new_vals, acc):
    s = pl.program_id(0)
    length = info[s, 0]
    added = info[s, 1]
    fresh = arr[:, pl.ds(pl.multiple_of(ZROWS + s * FRESH, FRESH), FRESH), :]
    fresh = fresh.reshape(XC * FRESH, W)
    pos = lax.broadcasted_iota(jnp.int32, (SEG, XC * FRESH), 0) - length
    j = lax.broadcasted_iota(jnp.int32, (SEG, XC * FRESH), 1)
    k = j % 4
    step = ((j // 4) % 4) * 16 + (j // 16) * 2
    rowpos = lax.broadcasted_iota(jnp.int32, (SEG, W), 0)
    fill = (rowpos >= length) & (rowpos < length + added)
    live = rowpos < length + added
    hot_k = ((pos == step + k) & (k < 2)).astype(F32).astype(BF)
    hot_v = ((pos == step + k - 2) & (k >= 2)).astype(F32).astype(BF)
    kk = jnp.where(
        fill, jnp.dot(hot_k, fresh, preferred_element_type=F32), keys[...].astype(F32)
    ).astype(BF)
    vv = jnp.where(
        fill, jnp.dot(hot_v, fresh, preferred_element_type=F32), vals[...].astype(F32)
    )
    new_keys[...] = kk
    new_vals[...] = vv.astype(BF)
    vz = jnp.where(live, vv, 0.0).astype(BF)
    row = lax.broadcasted_iota(jnp.int32, (XC * ZROWS, NZ * XC), 0)
    lane = lax.broadcasted_iota(jnp.int32, (XC * ZROWS, NZ * XC), 1)
    batch = ((row // MB) % NZ) * XC + row // ZROWS
    hot_b = (lane == batch).astype(F32).astype(BF)
    use = lax.dot_general(
        hot_b, maskrow[s], (((1,), (1,)), ((), ())), preferred_element_type=F32
    )
    for t in range(XC):
        lo = t * ZROWS
        use_t = use[lo : lo + ZROWS, 0:1]
        for h in range(HEADS):
            cs = slice(h * DH, (h + 1) * DH)
            logits = lax.dot_general(
                arr[t, 0:ZROWS, cs],
                kk[:, cs],
                (((1,), (1,)), ((), ())),
                preferred_element_type=F32,
            )
            e = jnp.exp2(logits * (-SCALE * LOG2E))
            wt = ((logits * SCALE) * pl.reciprocal(1.0 + e, approx=True)).astype(BF)
            o = jnp.dot(wt, vz[:, cs], preferred_element_type=F32) * use_t

            @pl.when(s == 0)
            def _():
                acc[lo : lo + ZROWS, cs] = o

            @pl.when(s == 1)
            def _():
                part[t, :, cs] = (acc[lo : lo + ZROWS, cs] + o).astype(BF)


def attend(info, maskrow, arr, keys, vals):
    rows = SEG_DEV * SEG
    return pl.pallas_call(
        attend_kernel,
        grid=(SEG_DEV,),
        out_shape=(
            jax.ShapeDtypeStruct((XC, ZROWS, W), BF),
            jax.ShapeDtypeStruct((rows, W), BF),
            jax.ShapeDtypeStruct((rows, W), BF),
        ),
        in_specs=[
            sspec(),
            pl.BlockSpec((SEG_DEV, 8, NZ * XC), lambda s: (0, 0, 0)),
            pl.BlockSpec((XC, PAY, W), lambda s: (0, 0, 0)),
            pl.BlockSpec((SEG, W), lambda s: (s, 0)),
            pl.BlockSpec((SEG, W), lambda s: (s, 0)),
        ],
        out_specs=(
            pl.BlockSpec((XC, ZROWS, W), lambda s: (0, 0, 0)),
            pl.BlockSpec((SEG, W), lambda s: (s, 0)),
            pl.BlockSpec((SEG, W), lambda s: (s, 0)),
        ),
        scratch_shapes=[pltpu.VMEM((XC * ZROWS, W), F32)],
        compiler_params=pltpu.CompilerParams(vmem_limit_bytes=32 * 1024 * 1024),
        name="attend",
    )(info, maskrow, arr, keys, vals)


def fold_kernel(arr, out):
    out[...] = jnp.sum(arr[...].astype(F32), axis=0).astype(BF)


def fold(arr):
    return pl.pallas_call(
        fold_kernel,
        out_shape=jax.ShapeDtypeStruct((ZROWS, W), BF),
        in_specs=[vspec()],
        out_specs=vspec(),
        name="fold",
    )(arr)


def two_terms(x):
    hi = x.astype(BF)
    lo = (x - hi.astype(F32)).astype(BF)
    return hi, lo


def gate_kernel(cand, wg, wo, gate, base):
    v = jnp.dot(cand[...], wg[...], preferred_element_type=F32)
    g = v / (1.0 + jnp.exp(-v))
    gate[...] = g
    hi, lo = two_terms(g)
    base[...] = jnp.dot(hi, wo[...], preferred_element_type=F32) + jnp.dot(
        lo, wo[...], preferred_element_type=F32
    )


def gate_and_base(cand, wg, wo):
    return pl.pallas_call(
        gate_kernel,
        out_shape=(
            jax.ShapeDtypeStruct((MB, W), F32),
            jax.ShapeDtypeStruct((MB, D), F32),
        ),
        in_specs=[vspec()] * 3,
        out_specs=(vspec(), vspec()),
        name="gate",
    )(cand, wg, wo)


MSG = 2 * W + 128


def mix_kernel(arr, gate, base, wo, out):
    att = jnp.sum(arr[...].astype(F32).reshape(NZ, MB, W), axis=0)
    mean = jnp.sum(att, axis=1, keepdims=True) * (1.0 / W)
    d = att - mean
    sq = jnp.sum(d * d, axis=1, keepdims=True)
    hi, lo = two_terms(d * gate[...])
    a = jnp.dot(hi, wo[...], preferred_element_type=F32) + jnp.dot(
        lo, wo[...], preferred_element_type=F32
    )
    b = base[...]
    lane = lax.broadcasted_iota(jnp.int32, (MB, 128), 1)
    stats = jnp.where(lane == 0, mean, sq)
    for i in range(MP):
        out[i, :, 0:W] = a[:, i * W : (i + 1) * W]
        out[i, :, W : 2 * W] = b[:, i * W : (i + 1) * W]
        out[i, :, 2 * W : MSG] = stats


def mix(arr, gate, base, wo):
    return pl.pallas_call(
        mix_kernel,
        out_shape=jax.ShapeDtypeStruct((MP, MB, MSG), F32),
        in_specs=[vspec()] * 4,
        out_specs=vspec(),
        name="mix",
    )(arr, gate, base, wo)


def finish_kernel(me, arr, cand, out):
    means = [arr[i, :, 2 * W : 2 * W + 1] for i in range(MP)]
    mean = sum(means) * (1.0 / MP)
    square = sum(arr[i, :, 2 * W + 1 : 2 * W + 2] for i in range(MP))
    square = square + W * sum((m - mean) * (m - mean) for m in means)
    scale = lax.rsqrt(square * (1.0 / D) + 1e-05)
    total = sum(
        arr[i, :, 0:W] + (means[i] - mean) * arr[i, :, W : 2 * W] for i in range(MP)
    )
    own = cand[:, pl.ds(pl.multiple_of(me[0] * W, W), W)].astype(F32)
    out[...] = (own + total * scale).astype(BF)


def finish(me, arr, cand):
    return pl.pallas_call(
        finish_kernel,
        out_shape=jax.ShapeDtypeStruct((MB, W), BF),
        in_specs=[sspec(), vspec(), vspec()],
        out_specs=vspec(),
        name="finish",
    )(me, arr, cand)


def exchange(x, axes):
    return lax.all_to_all(x, axes, split_axis=0, concat_axis=0, tiled=True)


def per_device(
    candidates,
    actions,
    hist_keys,
    hist_values,
    w_query,
    w_gate,
    w_key,
    w_value,
    w_out,
    segment_list,
    segment_count,
    segment_length,
    new_count,
    batch_user,
):
    z = lax.axis_index("z")
    device = z * XC + lax.axis_index("x") * NC + lax.axis_index("core")
    me = lax.axis_index("mp").astype(jnp.int32).reshape(1)
    user_ids = jnp.arange(USERS, dtype=jnp.int32)
    slots = jnp.arange(segment_list.shape[1], dtype=jnp.int32)
    last_segment = jnp.sum(
        jnp.where(slots[None, :] == (segment_count - 1)[:, None], segment_list, 0), axis=1
    )

    rows = jnp.arange(XC * SEG_DEV * FRESH, dtype=jnp.int32)
    row_seg = z * XC * SEG_DEV + rows // FRESH
    row_hot = row_seg[:, None] == last_segment[None, :]
    row_user = jnp.sum(jnp.where(row_hot, user_ids[None, :], 0), axis=1)
    row_col = (row_user * 4 + (rows // 4) % 4) * 8 + rows % 4
    row_col = jnp.where(jnp.any(row_hot, axis=1), row_col, -1)[:, None]

    own = device * SEG_DEV + jnp.arange(SEG_DEV, dtype=jnp.int32)
    own_hot = own[:, None] == last_segment[None, :]
    own_added = jnp.sum(jnp.where(own_hot, new_count[None, :], 0), axis=1)
    own_length = lax.dynamic_slice_in_dim(segment_length, device * SEG_DEV, SEG_DEV)
    info = jnp.stack([own_length, own_added], axis=1)
    listed = jnp.any(segment_list[None, :, :] == own[:, None, None], axis=2)
    owner = jnp.sum(jnp.where(listed, user_ids[None, :], 0), axis=1)
    mask = (batch_user[None, :] == owner[:, None]).astype(BF)
    mask = jnp.broadcast_to(mask[:, None, :], (SEG_DEV, 8, NZ * XC))

    with jax.named_scope("gather"):
        message = project(candidates, actions, w_query, w_key, w_value)
        arrived = exchange(message, "z")
        payload = spread(row_col, arrived)
        queries = exchange(payload, ("x", "core"))
    gate, base = gate_and_base(candidates, w_gate, w_out)
    with jax.named_scope("attend"):
        part, new_keys, new_values = attend(info, mask, queries, hist_keys, hist_values)
    with jax.named_scope("return"):
        part = exchange(part, ("x", "core"))
        part = fold(part)
        part = exchange(part, "z")
    with jax.named_scope("mix"):
        mixed = mix(part, gate, base, w_out)
        mixed = exchange(mixed, "mp")
        ranked = finish(me, mixed, candidates)
    return (ranked, new_keys, new_values)


def solution(mesh):
    names = ("z", "x", "core", "mp")
    inner = Mesh(mesh.devices.reshape(NZ, NX, NC, MP), names)
    hist = ("z", "x", "core")
    in_specs = (
        P(hist, None),
        P(hist, None),
        P(hist, "mp"),
        P(hist, "mp"),
        P(None, "mp"),
        P(None, "mp"),
        P(None, "mp"),
        P(None, "mp"),
        P("mp", None),
        P(),
        P(),
        P(),
        P(),
        P(),
    )
    out_specs = (P(hist, "mp"), P(hist, "mp"), P(hist, "mp"))
    return jax.shard_map(
        per_device, mesh=inner, in_specs=in_specs, out_specs=out_specs, check_vma=False
    )
```

```python
import functools
import math

import jax
import jax.numpy as jnp
from jax import lax
from jax.experimental import pallas as pl
from jax.experimental.pallas import tpu as pltpu
from jax.sharding import Mesh
from jax.sharding import PartitionSpec as P

D = 1024
DH = 128
SEG = 512
NEW = 64
USERS = 4
NZ = 16
NX = 4
NC = 2
XC = NX * NC
ZX = NZ * NX
MP = 4
MB = 8
SEG_DEV = 2
W = D // MP
HEADS = W // DH
BATCHES = NZ * XC
QROWS = BATCHES * MB
HALF = ZX * MB
ZROWS = NZ * MB
FIRST_Z = 12
ACT = 2
SCALE = 1.0 / math.sqrt(DH)
LOG2E = 1.4426950408889634
BF = jnp.bfloat16
F32 = jnp.float32
MIB = 1024 * 1024


def vspec():
    return pl.BlockSpec(memory_space=pltpu.VMEM)


def sspec():
    return pl.BlockSpec(memory_space=pltpu.SMEM)


def aspec():
    return pl.BlockSpec(memory_space=pl.ANY)


def params(mib):
    return pltpu.CompilerParams(vmem_limit_bytes=mib * MIB)


def cost(flops, nbytes):
    return pl.CostEstimate(flops=flops, bytes_accessed=nbytes, transcendentals=0)


def project_kernel(cand, act, wq, wk, wv, msg, kx, vx, c, a, q, k, v, block, sems):
    pairs = ((cand, c), (wq, q), (act, a), (wk, k), (wv, v))
    copies = [pltpu.make_async_copy(x, y, sems.at[i]) for i, (x, y) in enumerate(pairs)]
    for copy in copies:
        copy.start()
    block[...] = jnp.zeros_like(block)
    copies[0].wait()
    copies[1].wait()
    query = jnp.dot(c[...], q[...], preferred_element_type=F32).astype(BF)
    copies[2].wait()
    copies[3].wait()
    key = jnp.dot(a[...], k[...], preferred_element_type=F32)
    copies[4].wait()
    value = jnp.dot(a[...], v[...], preferred_element_type=F32)
    for h in range(HEADS):
        cs = slice(h * DH, (h + 1) * DH)
        block[h * 4 : h * 4 + 2, 0:DH] = key[:, cs]
        block[h * 4 + 2 : h * 4 + 4, 0:DH] = value[:, cs]
    fresh = block[0:MB, 0:DH].astype(BF)
    for i in range(NZ):
        msg[i, :, 0:W] = query
        msg[i, :, W : W + DH] = fresh
    block[0:MB, 0:DH] = jnp.zeros((MB, DH), F32)
    lane = lax.broadcasted_iota(jnp.int32, (ACT, W), 1)
    for src, dst in ((key, kx), (value, vx)):
        for h in range(HEADS):
            block[h * ACT : (h + 1) * ACT] = jnp.where(lane // DH == h, src, 0.0)
        dst[...] = block[...].astype(BF)


def project(cand, act, wq, wk, wv):
    weight = pltpu.VMEM((D, W), BF)
    return pl.pallas_call(
        project_kernel,
        out_shape=(
            jax.ShapeDtypeStruct((NZ, MB, W + DH), BF),
            jax.ShapeDtypeStruct((DH, W), BF),
            jax.ShapeDtypeStruct((DH, W), BF),
        ),
        in_specs=[aspec()] * 5,
        out_specs=(vspec(),) * 3,
        scratch_shapes=[
            pltpu.VMEM((MB, D), BF),
            pltpu.VMEM((ACT, D), BF),
            weight,
            weight,
            weight,
            pltpu.VMEM((DH, W), F32),
            pltpu.SemaphoreType.DMA((5,)),
        ],
        name="project",
    )(cand, act, wq, wk, wv)


def spread_kernel(arr, out):
    rows = arr[...]
    for t in range(NX):
        out[t] = rows


def spread(arr):
    return pl.pallas_call(
        spread_kernel,
        out_shape=jax.ShapeDtypeStruct((NX, ZROWS, W + DH), BF),
        in_specs=[vspec()],
        out_specs=vspec(),
        compiler_params=params(8),
        name="spread",
    )(arr)


BLOCK = 512
PATCH = NEW + 16


def attend_kernel(
    info, maskrow, arr, kx, vx, keys, vals, part, new_keys, new_vals, patch, sems
):
    pairs = ((keys, new_keys), (vals, new_vals))
    copies = [pltpu.make_async_copy(x, y, sems.at[i]) for i, (x, y) in enumerate(pairs)]
    for copy in copies:
        copy.start()

    shape = (PATCH, XC * 4 * MB)
    j = lax.broadcasted_iota(jnp.int32, shape, 1)
    source = ((j // 32) % NX) * NC + j // 128
    step = ((j // 8) % 4) * 16 + source * 2 + j % 2
    kind = (j // 2) % 4
    patches = []
    for s in range(SEG_DEV):
        length = info[s, 0]
        added = info[s, 1]
        start = ((info[s, 2] * 4 + (NZ - FIRST_Z)) % NZ) * MB
        begin = pl.multiple_of(jnp.minimum((length // 16) * 16, SEG - PATCH), 16)
        fresh = arr[:, pl.ds(pl.multiple_of(start, 4 * MB), 4 * MB), W : W + DH]
        fresh = fresh.reshape(XC * 4 * MB, DH)
        pos = lax.broadcasted_iota(jnp.int32, shape, 0) + (begin - length)
        rowpos = lax.broadcasted_iota(jnp.int32, (PATCH, DH), 0) + (begin - length)
        fill = (rowpos >= 0) & (rowpos < added)
        rows = pl.ds(pl.multiple_of(s * SEG + begin, 16), PATCH)
        for i, (old, new) in enumerate(pairs):
            slot = s * 2 + i
            for h in range(HEADS):
                cs = slice(h * DH, (h + 1) * DH)
                hot = ((pos == step) & (kind == 2 * h + i)).astype(F32).astype(BF)
                placed = jnp.dot(hot, fresh, preferred_element_type=F32)
                kept = old[rows, cs].astype(F32)
                patch[slot, :, cs] = jnp.where(fill, placed, kept).astype(BF)
            patches.append(
                pltpu.make_async_copy(patch.at[slot], new.at[rows], sems.at[2 + slot])
            )

    row = lax.broadcasted_iota(jnp.int32, (QROWS, BATCHES), 0)
    lane = lax.broadcasted_iota(jnp.int32, (QROWS, BATCHES), 1)
    step = (row % ZROWS) // MB
    group = row // ZROWS
    batch = ((step + FIRST_Z) % NZ) * XC + (group % NX) * NC + group // NX
    hot = (lane == batch).astype(F32).astype(BF)
    use = lax.dot_general(
        hot, maskrow[...], (((1,), (1,)), ((), ())), preferred_element_type=F32
    )
    rowpos = lax.broadcasted_iota(jnp.int32, (SEG, W), 0)
    zero = jnp.zeros((), BF)
    live = []
    for s in range(SEG_DEV):
        v = vals[s * SEG : (s + 1) * SEG].astype(F32)
        live.append(jnp.where(rowpos < info[s, 0], v, 0.0).astype(BF))

    fresh = lax.broadcasted_iota(jnp.int32, (DH, W), 0) % ACT
    own = jnp.where(fresh < info[SEG_DEV, 0], vx[...].astype(F32), 0.0).astype(BF)

    def weigh(logits):
        e = jnp.exp2(logits * (-SCALE * LOG2E))
        return ((logits * SCALE) * pl.reciprocal(1.0 + e, approx=True)).astype(BF)

    def score(a, b):
        return lax.dot_general(a, b, (((1,), (1,)), ((), ())), preferred_element_type=F32)

    for r in range(0, QROWS, BLOCK):
        if r == BLOCK:
            for copy in copies:
                copy.wait()
            for copy in patches:
                copy.start()
        first = r // ZROWS
        qr = arr[first : first + BLOCK // ZROWS, :, 0:W].reshape(BLOCK, W)
        wx = weigh(score(qr, kx[...]))
        ox = jnp.dot(wx, own, preferred_element_type=F32) * use[r : r + BLOCK, 2:3]
        for h in range(HEADS):
            cs = slice(h * DH, (h + 1) * DH)
            total = ox[:, cs]
            for s in range(SEG_DEV):
                wt = weigh(score(qr[:, cs], keys[s * SEG : (s + 1) * SEG, cs]))
                o = jnp.dot(wt, live[s][:, cs], preferred_element_type=F32)
                total = total + o * use[r : r + BLOCK, s : s + 1]
            total = total.astype(BF)
            for i in range(BLOCK // ZROWS):
                group = r // ZROWS + i
                lo = i * ZROWS
                part[(group % NX) * NC + group // NX, :, cs] = total[lo : lo + ZROWS]
    for copy in patches:
        copy.wait()


def attend(info, maskrow, arr, kx, vx, keys, vals):
    stored = jax.ShapeDtypeStruct((SEG_DEV * SEG, W), BF)
    return pl.pallas_call(
        attend_kernel,
        out_shape=(jax.ShapeDtypeStruct((XC, ZROWS, W), BF), stored, stored),
        in_specs=[sspec()] + [vspec()] * 6,
        out_specs=(vspec(), aspec(), aspec()),
        scratch_shapes=[
            pltpu.VMEM((SEG_DEV * 2, PATCH, W), BF),
            pltpu.SemaphoreType.DMA((2 + SEG_DEV * 2,)),
        ],
        compiler_params=params(32),
        name="attend",
    )(info, maskrow, arr, kx, vx, keys, vals)


def fold_kernel(arr, out):
    out[...] = jnp.sum(arr[...].astype(F32), axis=0).astype(BF)


def fold(arr):
    return pl.pallas_call(
        fold_kernel,
        out_shape=jax.ShapeDtypeStruct((ZROWS, W), BF),
        in_specs=[vspec()],
        out_specs=vspec(),
        compiler_params=params(8),
        name="fold",
    )(arr)


def two_terms(x):
    hi = x.astype(BF)
    lo = (x - hi.astype(F32)).astype(BF)
    return hi, lo


def gate_kernel(cand, wg, wo, gate, base):
    v = jnp.dot(cand[...], wg[...], preferred_element_type=F32)
    g = v / (1.0 + jnp.exp(-v))
    gate[...] = g
    hi, lo = two_terms(g)
    base[...] = jnp.dot(hi, wo[...], preferred_element_type=F32) + jnp.dot(
        lo, wo[...], preferred_element_type=F32
    )


def gate_and_base(cand, wg, wo):
    return pl.pallas_call(
        gate_kernel,
        out_shape=(
            jax.ShapeDtypeStruct((MB, W), F32),
            jax.ShapeDtypeStruct((MB, D), F32),
        ),
        in_specs=[vspec()] * 3,
        out_specs=(vspec(), vspec()),
        compiler_params=params(8),
        cost_estimate=cost(10_000_000, 1_200_000),
        name="gate",
    )(cand, wg, wo)


MSG = 2 * W + 128


def mix_kernel(arr, gate, base, wo, out):
    att = jnp.sum(arr[...].astype(F32).reshape(NZ, MB, W), axis=0)
    mean = jnp.sum(att, axis=1, keepdims=True) * (1.0 / W)
    d = att - mean
    sq = jnp.sum(d * d, axis=1, keepdims=True)
    hi, lo = two_terms(d * gate[...])
    a = jnp.dot(hi, wo[...], preferred_element_type=F32) + jnp.dot(
        lo, wo[...], preferred_element_type=F32
    )
    b = base[...]
    lane = lax.broadcasted_iota(jnp.int32, (MB, 128), 1)
    stats = jnp.where(lane == 0, mean, sq)
    for i in range(MP):
        out[i, :, 0:W] = a[:, i * W : (i + 1) * W]
        out[i, :, W : 2 * W] = b[:, i * W : (i + 1) * W]
        out[i, :, 2 * W : MSG] = stats


def mix(arr, gate, base, wo):
    return pl.pallas_call(
        mix_kernel,
        out_shape=jax.ShapeDtypeStruct((MP, MB, MSG), F32),
        in_specs=[vspec()] * 4,
        out_specs=vspec(),
        compiler_params=params(8),
        name="mix",
    )(arr, gate, base, wo)


def finish_kernel(me, arr, cand, out):
    means = [arr[i, :, 2 * W : 2 * W + 1] for i in range(MP)]
    mean = sum(means) * (1.0 / MP)
    square = sum(arr[i, :, 2 * W + 1 : 2 * W + 2] for i in range(MP))
    square = square + W * sum((m - mean) * (m - mean) for m in means)
    scale = lax.rsqrt(square * (1.0 / D) + 1e-05)
    total = sum(
        arr[i, :, 0:W] + (means[i] - mean) * arr[i, :, W : 2 * W] for i in range(MP)
    )
    own = cand[:, pl.ds(pl.multiple_of(me[0] * W, W), W)].astype(F32)
    out[...] = (own + total * scale).astype(BF)


def finish(me, arr, cand):
    return pl.pallas_call(
        finish_kernel,
        out_shape=jax.ShapeDtypeStruct((MB, W), BF),
        in_specs=[sspec(), vspec(), vspec()],
        out_specs=vspec(),
        compiler_params=params(8),
        name="finish",
    )(me, arr, cand)


def exchange(x, axes):
    groups = [[(i + FIRST_Z) % NZ for i in range(NZ)]] if axes == "z" else None
    return lax.all_to_all(
        x, axes, split_axis=0, concat_axis=0, tiled=True, axis_index_groups=groups
    )


def per_device(
    candidates,
    actions,
    hist_keys,
    hist_values,
    w_query,
    w_gate,
    w_key,
    w_value,
    w_out,
    segment_list,
    segment_count,
    segment_length,
    new_count,
    batch_user,
):
    z = lax.axis_index("z").astype(jnp.int32)
    core = lax.axis_index("core").astype(jnp.int32)
    device = z * XC + lax.axis_index("x").astype(jnp.int32) * NC + core
    me = lax.axis_index("mp").astype(jnp.int32).reshape(1)
    user_ids = jnp.arange(USERS, dtype=jnp.int32)
    slots = jnp.arange(segment_list.shape[1], dtype=jnp.int32)
    last_segment = jnp.sum(
        jnp.where(slots[None, :] == (segment_count - 1)[:, None], segment_list, 0), axis=1
    )

    own = device * SEG_DEV + jnp.arange(SEG_DEV, dtype=jnp.int32)
    own_hot = own[:, None] == last_segment[None, :]
    own_added = jnp.sum(jnp.where(own_hot, new_count[None, :], 0), axis=1)
    own_user = jnp.sum(jnp.where(own_hot, user_ids[None, :], 0), axis=1)
    own_length = lax.dynamic_slice_in_dim(segment_length, device * SEG_DEV, SEG_DEV)
    listed = jnp.any(segment_list[None, :, :] == own[:, None, None], axis=2)
    owner = jnp.sum(jnp.where(listed, user_ids[None, :], 0), axis=1)

    act_user = device * ACT // NEW
    act_count = jnp.sum(jnp.where(user_ids == act_user, new_count, 0))
    act_valid = jnp.clip(act_count - device * ACT % NEW, 0, ACT)
    nothing = jnp.zeros((), jnp.int32)
    info = jnp.stack(
        [
            jnp.append(own_length, act_valid),
            jnp.append(own_added, nothing),
            jnp.append(own_user, nothing),
        ],
        axis=1,
    )
    mask_user = jnp.concatenate([owner, jnp.broadcast_to(act_user, (6,))])
    mask = (batch_user[None, :] == mask_user[:, None]).astype(BF)

    with jax.named_scope("gather"):
        message, key_block, value_block = project(
            candidates, actions, w_query, w_key, w_value
        )
        arrived = exchange(message, "z")
        gate, base = gate_and_base(candidates, w_gate, w_out)
        arrived, gate, base, info, mask, me = lax.optimization_barrier(
            (arrived, gate, base, info, mask, me)
        )
        arrived = exchange(spread(arrived.reshape(ZROWS, W + DH)), "x")
        arrived = lax.all_gather(arrived, "core", axis=0)
    with jax.named_scope("attend"):
        part, new_keys, new_values = attend(
            info,
            mask,
            arrived.reshape(XC, ZROWS, W + DH),
            key_block,
            value_block,
            hist_keys,
            hist_values,
        )
    with jax.named_scope("return"):
        part = fold(exchange(part, ("x", "core")))
        summed = exchange(part, "z")
    with jax.named_scope("mix"):
        mixed = mix(summed, gate, base, w_out)
        mixed = exchange(mixed, "mp")
        ranked = finish(me, mixed, candidates)
    return (ranked, new_keys, new_values)


def solution(mesh):
    names = ("z", "x", "core", "mp")
    inner = Mesh(mesh.devices.reshape(NZ, NX, NC, MP), names)
    hist = ("z", "x", "core")
    in_specs = (
        P(hist, None),
        P(hist, None),
        P(hist, "mp"),
        P(hist, "mp"),
        P(None, "mp"),
        P(None, "mp"),
        P(None, "mp"),
        P(None, "mp"),
        P("mp", None),
        P(),
        P(),
        P(),
        P(),
        P(),
    )
    out_specs = (P(hist, "mp"), P(hist, "mp"), P(hist, "mp"))
    return jax.shard_map(
        per_device, mesh=inner, in_specs=in_specs, out_specs=out_specs, check_vma=False
    )
```

```python
import functools
import math

import jax
import jax.numpy as jnp
from jax import lax
from jax.experimental import pallas as pl
from jax.experimental.pallas import tpu as pltpu
from jax.sharding import Mesh
from jax.sharding import PartitionSpec as P

D = 1024
DH = 128
SEG = 512
NEW = 64
USERS = 4
NZ = 16
NX = 4
NC = 2
XC = NX * NC
ZX = NZ * NX
MP = 4
MB = 8
SEG_DEV = 2
W = D // MP
HEADS = W // DH
BATCHES = NZ * XC
QROWS = BATCHES * MB
HALF = ZX * MB
ZROWS = NZ * MB
FIRST_Z = 8
RETURN_Z = 8
TURN = (FIRST_Z - RETURN_Z) % NZ * MB
STORED = SEG_DEV * SEG
OWN = 16
ACT = 2
SCALE = 1.0 / math.sqrt(DH)
LOG2E = 1.4426950408889634
BF = jnp.bfloat16
F32 = jnp.float32
MIB = 1024 * 1024


def vspec():
    return pl.BlockSpec(memory_space=pltpu.VMEM)


def sspec():
    return pl.BlockSpec(memory_space=pltpu.SMEM)


def aspec():
    return pl.BlockSpec(memory_space=pl.ANY)


def params(mib):
    return pltpu.CompilerParams(vmem_limit_bytes=mib * MIB)


def cost(flops, nbytes):
    return pl.CostEstimate(flops=flops, bytes_accessed=nbytes, transcendentals=0)


def place():
    core = lax.axis_index("core")
    return core, lax.axis_index("z") * XC + lax.axis_index("x") * NC + core


def project_kernel(*refs):
    small, big, outs = refs[:5], refs[5:10], refs[10:14]
    scalars, vectors, weights = refs[14:18], refs[18:20], refs[20:25]
    rows, block, marks, sems = refs[25:]
    msg, own, info, mask = outs
    heavy = [pltpu.make_async_copy(x, y, sems.at[i]) for i, (x, y) in enumerate(zip(big, weights))]
    sources = small[:4] + (small[0], small[4])
    light = [
        pltpu.make_async_copy(x, y, sems.at[5 + i])
        for i, (x, y) in enumerate(zip(sources, scalars + vectors))
    ]
    for copy in heavy[:2] + light + heavy[2:]:
        copy.start()
    block[...] = jnp.zeros_like(block)
    marks[...] = jnp.zeros_like(marks)
    for copy in light:
        copy.wait()

    lists, counts, lengths, news = scalars
    core, device = place()
    ends = [lists[u, counts[u] - 1] for u in range(USERS)]
    for s in range(SEG_DEV):
        segment = device * SEG_DEV + s
        added = jnp.int32(0)
        user = jnp.int32(0)
        for u in range(USERS):
            hit = ends[u] == segment
            added = jnp.where(hit, news[u], added)
            user = jnp.where(hit, u, user)
        info[s, 0] = lengths[segment]
        info[s, 1] = added
        info[s, 2] = user

    act_user = device * ACT // NEW
    listed = vectors[0][...]
    listing = lax.broadcasted_iota(jnp.int32, listed.shape, 0).astype(F32)
    users = vectors[1][...]
    batch = users.astype(F32)
    for c in range(NC):
        near = device if c == 0 else device + 1 - 2 * core
        for s in range(SEG_DEV):
            hit = listed == near * SEG_DEV + s
            owner = jnp.sum(jnp.where(hit, listing, 0.0), axis=0, keepdims=True)
            owner = jnp.sum(owner, axis=1, keepdims=True)
            k = c * SEG_DEV + s
            marks[k : k + 1] = jnp.where(batch == owner, 1.0, 0.0)
    marks[4:5] = jnp.where(users == act_user, 1.0, 0.0)
    mask[...] = marks[...].astype(BF)

    c, q, a, k, v = weights
    heavy[0].wait()
    heavy[1].wait()
    query = jnp.dot(c[...], q[...], preferred_element_type=F32).astype(BF)
    heavy[2].wait()
    heavy[3].wait()
    key = jnp.dot(a[...], k[...], preferred_element_type=F32)
    heavy[4].wait()
    value = jnp.dot(a[...], v[...], preferred_element_type=F32)
    block[0:2] = key
    block[2:4] = value
    for h in range(HEADS):
        rows[h * 4 : h * 4 + 4] = block[0:4, h * DH : (h + 1) * DH]
    fresh = rows[...].astype(BF)
    for i in range(NZ):
        msg[i, :, 0:W] = query
        msg[i, :, W : W + DH] = fresh
    valid = jnp.clip(news[act_user] - device * ACT % NEW, 0, ACT)
    row = lax.broadcasted_iota(jnp.int32, (ACT, W), 0)
    block[2:4] = jnp.where(row < valid, value, 0.0)
    own[...] = block[...].astype(BF)


def project(lists, counts, lengths, news, users, cand, act, wq, wk, wv):
    weight = pltpu.VMEM((D, W), BF)
    return pl.pallas_call(
        project_kernel,
        out_shape=(
            jax.ShapeDtypeStruct((NZ, MB, W + DH), BF),
            jax.ShapeDtypeStruct((OWN, W), BF),
            jax.ShapeDtypeStruct((SEG_DEV, 3), jnp.int32),
            jax.ShapeDtypeStruct((8, BATCHES), BF),
        ),
        in_specs=[aspec()] * 10,
        out_specs=(vspec(), vspec(), sspec(), vspec()),
        scratch_shapes=[
            pltpu.SMEM(lists.shape, jnp.int32),
            pltpu.SMEM(counts.shape, jnp.int32),
            pltpu.SMEM(lengths.shape, jnp.int32),
            pltpu.SMEM(news.shape, jnp.int32),
            pltpu.VMEM(lists.shape, jnp.int32),
            pltpu.VMEM((1, BATCHES), jnp.int32),
            pltpu.VMEM((MB, D), BF),
            weight,
            pltpu.VMEM((ACT, D), BF),
            weight,
            weight,
            pltpu.VMEM((MB, DH), F32),
            pltpu.VMEM((OWN, W), F32),
            pltpu.VMEM((8, BATCHES), F32),
            pltpu.SemaphoreType.DMA((11,)),
        ],
        name="project",
    )(lists, counts, lengths, news, users.reshape(1, BATCHES), cand, wq, act, wk, wv)


def stage_kernel(info, own, keys, vals, out):
    out[0:STORED] = keys[...]
    rowpos = lax.broadcasted_iota(jnp.int32, (SEG, W), 0)
    for s in range(SEG_DEV):
        v = vals[s * SEG : (s + 1) * SEG].astype(F32)
        lo = STORED + s * SEG
        out[lo : lo + SEG] = jnp.where(rowpos < info[s, 0], v, 0.0).astype(BF)
    out[2 * STORED :] = own[...]


def stage(info, own, keys, vals):
    return pl.pallas_call(
        stage_kernel,
        out_shape=jax.ShapeDtypeStruct((2 * STORED + OWN, W), BF),
        in_specs=[sspec()] + [vspec()] * 3,
        out_specs=vspec(),
        compiler_params=params(16),
        cost_estimate=cost(1_000_000, 2_200_000),
        name="stage",
    )(info, own, keys, vals)


def spread_kernel(arr, out):
    rows = arr[...]
    for t in range(NX):
        out[t] = rows


def spread(arr):
    return pl.pallas_call(
        spread_kernel,
        out_shape=jax.ShapeDtypeStruct((NX, ZROWS, W + DH), BF),
        in_specs=[vspec()],
        out_specs=vspec(),
        compiler_params=params(8),
        name="spread",
    )(arr)


def append_kernel(info, arr, keys, vals, new_keys, new_vals):
    s = pl.program_id(0)
    length = info[s, 0]
    added = info[s, 1]
    user = info[s, 2]
    start = ((user * 4 + (NZ - FIRST_Z)) % NZ) * MB
    fresh = arr[:, pl.ds(pl.multiple_of(start, 4 * MB), 4 * MB), :].reshape(XC * 4 * MB, DH)
    shape = (SEG, XC * 4 * MB)
    pos = lax.broadcasted_iota(jnp.int32, shape, 0) - length
    j = lax.broadcasted_iota(jnp.int32, shape, 1)
    source = ((j // 32) % NX) * NC + j // 128
    step = ((j // 8) % 4) * 16 + source * 2 + j % 2
    kind = (j // 2) % 4
    rowpos = lax.broadcasted_iota(jnp.int32, (SEG, DH), 0)
    fill = (rowpos >= length) & (rowpos < length + added)
    for h in range(HEADS):
        cs = slice(h * DH, (h + 1) * DH)
        for i, (old, new) in enumerate(((keys, new_keys), (vals, new_vals))):
            hot = ((pos == step) & (kind == 2 * h + i)).astype(F32).astype(BF)
            placed = jnp.dot(hot, fresh, preferred_element_type=F32)
            new[:, cs] = jnp.where(fill, placed, old[:, cs].astype(F32)).astype(BF)


def append(info, arr, keys, vals):
    rows = SEG_DEV * SEG
    block = pl.BlockSpec((SEG, W), lambda s: (s, 0))
    return pl.pallas_call(
        append_kernel,
        grid=(SEG_DEV,),
        out_shape=(jax.ShapeDtypeStruct((rows, W), BF),) * 2,
        in_specs=[sspec(), pl.BlockSpec((XC, ZROWS, DH), lambda s: (0, 0, 0)), block, block],
        out_specs=(block, block),
        compiler_params=params(16),
        cost_estimate=cost(150_000_000, 2_500_000),
        name="append",
    )(info, arr, keys, vals)


def attend_kernel(maskrow, arr, mine, other, part, fresh, theirs, total, kx, vx, sem):
    copy = pltpu.make_async_copy(other, theirs, sem)
    copy.start()
    fresh[...] = arr[:, :, W:]
    shape = (HALF, BATCHES)
    row = lax.broadcasted_iota(jnp.int32, shape, 0)
    lane = lax.broadcasted_iota(jnp.int32, shape, 1)
    step = (row % ZROWS) // MB
    batch = ((step + FIRST_Z) % NZ) * XC + (row // ZROWS) * NC + lax.axis_index("core")
    hot = (lane == batch).astype(F32).astype(BF)
    use = lax.dot_general(
        hot, maskrow[...], (((1,), (1,)), ((), ())), preferred_element_type=F32
    )

    def weigh(logits):
        e = jnp.exp2(logits * (-SCALE * LOG2E))
        return (logits * SCALE) * pl.reciprocal(1.0 + e, approx=True)

    def score(a, b):
        return lax.dot_general(a, b, (((1,), (1,)), ((), ())), preferred_element_type=F32)

    def stored(c, src, h):
        cs = slice(h * DH, (h + 1) * DH)
        logits = score(q[:, cs], src[0:STORED, cs])
        parts = []
        for s in range(SEG_DEV):
            u = c * SEG_DEV + s
            seg = weigh(logits[:, s * SEG : (s + 1) * SEG]) * use[:, u : u + 1]
            parts.append(seg.astype(BF))
        wt = jnp.concatenate(parts, axis=1)
        return jnp.dot(wt, src[STORED : 2 * STORED, cs], preferred_element_type=F32)

    q = arr[:, :, 0:W].reshape(HALF, W)
    for h in range(HEADS):
        total[:, h * DH : (h + 1) * DH] = stored(0, mine, h)
    copy.wait()

    kx[...] = jnp.zeros_like(kx)
    vx[...] = jnp.zeros_like(vx)
    column = lax.broadcasted_iota(jnp.int32, (ACT, W), 1) // DH
    for c, src in enumerate((mine, theirs)):
        own = src[2 * STORED :].astype(F32)
        for h in range(HEADS):
            lo = (c * HEADS + h) * ACT
            kx[lo : lo + ACT] = jnp.where(column == h, own[0:ACT], 0.0)
            vx[lo : lo + ACT] = jnp.where(column == h, own[ACT : 2 * ACT], 0.0)
    wx = weigh(score(q, kx[...].astype(BF))) * use[:, 4:5]
    ox = jnp.dot(wx.astype(BF), vx[...].astype(BF), preferred_element_type=F32)
    for h in range(HEADS):
        cs = slice(h * DH, (h + 1) * DH)
        out = (total[:, cs] + stored(1, theirs, h) + ox[:, cs]).astype(BF)
        for x in range(NX):
            lo = x * ZROWS
            hi = lo + ZROWS
            part[x, TURN:, cs] = out[lo : hi - TURN]
            if TURN:
                part[x, 0:TURN, cs] = out[hi - TURN : hi]


def attend(maskrow, arr, mine, theirs):
    return pl.pallas_call(
        attend_kernel,
        out_shape=(
            jax.ShapeDtypeStruct((NX, ZROWS, W), BF),
            jax.ShapeDtypeStruct((NX, ZROWS, DH), BF),
        ),
        in_specs=[vspec()] * 3 + [aspec()],
        out_specs=(vspec(),) * 2,
        scratch_shapes=[
            pltpu.VMEM((2 * STORED + OWN, W), BF),
            pltpu.VMEM((HALF, W), F32),
            pltpu.VMEM((DH, W), F32),
            pltpu.VMEM((DH, W), F32),
            pltpu.SemaphoreType.DMA,
        ],
        compiler_params=params(32),
        name="attend",
    )(maskrow, arr, mine, theirs)


def fold_kernel(arr, out):
    out[...] = jnp.sum(arr[...].astype(F32), axis=0).astype(BF)


def fold(arr):
    return pl.pallas_call(
        fold_kernel,
        out_shape=jax.ShapeDtypeStruct((ZROWS, W), BF),
        in_specs=[vspec()],
        out_specs=vspec(),
        compiler_params=params(8),
        name="fold",
    )(arr)


def two_terms(x):
    hi = x.astype(BF)
    lo = (x - hi.astype(F32)).astype(BF)
    return hi, lo


def gate_kernel(cand, wg, wo, gate, base, own):
    first = pl.multiple_of(lax.axis_index("mp") * W, W)
    own[...] = cand[:, pl.ds(first, W)].astype(F32)
    v = jnp.dot(cand[...], wg[...], preferred_element_type=F32)
    g = v / (1.0 + jnp.exp(-v))
    gate[...] = g
    hi, lo = two_terms(g)
    base[...] = jnp.dot(hi, wo[...], preferred_element_type=F32) + jnp.dot(
        lo, wo[...], preferred_element_type=F32
    )


def gate_and_base(cand, wg, wo):
    return pl.pallas_call(
        gate_kernel,
        out_shape=(
            jax.ShapeDtypeStruct((MB, W), F32),
            jax.ShapeDtypeStruct((MB, D), F32),
            jax.ShapeDtypeStruct((MB, W), F32),
        ),
        in_specs=[vspec()] * 3,
        out_specs=(vspec(),) * 3,
        compiler_params=params(8),
        cost_estimate=cost(10_000_000_000, 40_000_000),
        name="gate",
    )(cand, wg, wo)


MSG = 2 * W + 128


def mix_kernel(arr, gate, base, wo, out):
    att = jnp.sum(arr[...].astype(F32).reshape(NZ, MB, W), axis=0)
    mean = jnp.sum(att, axis=1, keepdims=True) * (1.0 / W)
    d = att - mean
    sq = jnp.sum(d * d, axis=1, keepdims=True)
    hi, lo = two_terms(d * gate[...])
    a = jnp.dot(hi, wo[...], preferred_element_type=F32) + jnp.dot(
        lo, wo[...], preferred_element_type=F32
    )
    b = base[...]
    lane = lax.broadcasted_iota(jnp.int32, (MB, 128), 1)
    stats = jnp.where(lane == 0, mean, sq)
    for i in range(MP):
        out[i, :, 0:W] = a[:, i * W : (i + 1) * W]
        out[i, :, W : 2 * W] = b[:, i * W : (i + 1) * W]
        out[i, :, 2 * W : MSG] = stats


def mix(arr, gate, base, wo):
    return pl.pallas_call(
        mix_kernel,
        out_shape=jax.ShapeDtypeStruct((MP, MB, MSG), F32),
        in_specs=[vspec()] * 4,
        out_specs=vspec(),
        compiler_params=params(8),
        name="mix",
    )(arr, gate, base, wo)


def finish_kernel(arr, own, out):
    means = [arr[i, :, 2 * W : 2 * W + 1] for i in range(MP)]
    mean = sum(means) * (1.0 / MP)
    square = sum(arr[i, :, 2 * W + 1 : 2 * W + 2] for i in range(MP))
    square = square + W * sum((m - mean) * (m - mean) for m in means)
    scale = lax.rsqrt(square * (1.0 / D) + 1e-05)
    total = sum(
        arr[i, :, 0:W] + (means[i] - mean) * arr[i, :, W : 2 * W] for i in range(MP)
    )
    out[...] = (own[...] + total * scale).astype(BF)


def finish(arr, own):
    return pl.pallas_call(
        finish_kernel,
        out_shape=jax.ShapeDtypeStruct((MB, W), BF),
        in_specs=[vspec()] * 2,
        out_specs=vspec(),
        compiler_params=params(8),
        name="finish",
    )(arr, own)


def exchange(x, axes, first=None):
    groups = None if first is None else [[(i + first) % NZ for i in range(NZ)]]
    return lax.all_to_all(
        x, axes, split_axis=0, concat_axis=0, tiled=True, axis_index_groups=groups
    )


def per_device(
    candidates,
    actions,
    hist_keys,
    hist_values,
    w_query,
    w_gate,
    w_key,
    w_value,
    w_out,
    segment_list,
    segment_count,
    segment_length,
    new_count,
    batch_user,
):
    with jax.named_scope("gather"):
        message, own, info, mask = project(
            segment_list,
            segment_count,
            segment_length,
            new_count,
            batch_user,
            candidates,
            actions,
            w_query,
            w_key,
            w_value,
        )
        arrived = exchange(message, "z", FIRST_Z)
    with jax.named_scope("share"):
        mine = stage(info, own, hist_keys, hist_values)
        theirs = lax.ppermute(mine, "core", [(0, 1), (1, 0)])
        gate, base, residual = gate_and_base(candidates, w_gate, w_out)
        arrived, gate, base, residual = lax.optimization_barrier(
            (arrived, gate, base, residual)
        )
    with jax.named_scope("gather"):
        arrived = exchange(spread(arrived.reshape(ZROWS, W + DH)), "x")
    with jax.named_scope("attend"):
        part, fresh = attend(mask, arrived, mine, theirs)
    with jax.named_scope("return"):
        part = exchange(part, "x")
    with jax.named_scope("append"):
        fresh = lax.all_gather(fresh, "core", axis=0).reshape(XC, ZROWS, DH)
        new_keys, new_values = append(info, fresh, hist_keys, hist_values)
    with jax.named_scope("return"):
        part, new_keys, new_values = lax.optimization_barrier((part, new_keys, new_values))
        summed = exchange(fold(part), "z", RETURN_Z)
    with jax.named_scope("mix"):
        mixed = exchange(mix(summed, gate, base, w_out), "mp")
        ranked = finish(mixed, residual)
    return (ranked, new_keys, new_values)


def solution(mesh):
    names = ("z", "x", "core", "mp")
    inner = Mesh(mesh.devices.reshape(NZ, NX, NC, MP), names)
    hist = ("z", "x", "core")
    in_specs = (
        P(hist, None),
        P(hist, None),
        P(hist, "mp"),
        P(hist, "mp"),
        P(None, "mp"),
        P(None, "mp"),
        P(None, "mp"),
        P(None, "mp"),
        P("mp", None),
        P(),
        P(),
        P(),
        P(),
        P(),
    )
    out_specs = (P(hist, "mp"), P(hist, "mp"), P(hist, "mp"))
    return jax.shard_map(
        per_device, mesh=inner, in_specs=in_specs, out_specs=out_specs, check_vma=False
    )
```

```python
import functools
import math

import jax
import jax.numpy as jnp
from jax import lax
from jax.experimental import pallas as pl
from jax.experimental.pallas import tpu as pltpu
from jax.sharding import Mesh
from jax.sharding import PartitionSpec as P

D = 1024
DH = 128
SEG = 512
NEW = 64
USERS = 4
NZ = 16
NX = 4
NC = 2
XC = NX * NC
ZX = NZ * NX
MP = 4
MB = 8
SEG_DEV = 2
W = D // MP
HEADS = W // DH
BATCHES = NZ * XC
QROWS = BATCHES * MB
HALF = ZX * MB
ZROWS = NZ * MB
FIRST_Z = 8
FIRST_X = 2
FIRST_Y = 3
STORED = SEG_DEV * SEG
OWN = 16
ACT = 2
SCALE = 1.0 / math.sqrt(DH)
LOG2E = 1.4426950408889634
BF = jnp.bfloat16
F32 = jnp.float32
MIB = 1024 * 1024


def vspec():
    return pl.BlockSpec(memory_space=pltpu.VMEM)


def sspec():
    return pl.BlockSpec(memory_space=pltpu.SMEM)


def aspec():
    return pl.BlockSpec(memory_space=pl.ANY)


def params(mib):
    return pltpu.CompilerParams(vmem_limit_bytes=mib * MIB)


def cost(flops, nbytes):
    return pl.CostEstimate(flops=flops, bytes_accessed=nbytes, transcendentals=0)


def place():
    core = lax.axis_index("core")
    return core, lax.axis_index("z") * XC + lax.axis_index("x") * NC + core


def project_kernel(*refs):
    small, big, outs = refs[:5], refs[5:10], refs[10:14]
    scalars, vectors, weights = refs[14:18], refs[18:20], refs[20:25]
    rows, block, marks, sems = refs[25:]
    msg, own, info, mask = outs
    heavy = [pltpu.make_async_copy(x, y, sems.at[i]) for i, (x, y) in enumerate(zip(big, weights))]
    sources = small[:4] + (small[0], small[4])
    light = [
        pltpu.make_async_copy(x, y, sems.at[5 + i])
        for i, (x, y) in enumerate(zip(sources, scalars + vectors))
    ]
    for copy in heavy[:2] + light + heavy[2:]:
        copy.start()
    block[...] = jnp.zeros_like(block)
    marks[...] = jnp.zeros_like(marks)
    for copy in light:
        copy.wait()

    lists, counts, lengths, news = scalars
    core, device = place()
    ends = [lists[u, counts[u] - 1] for u in range(USERS)]
    for s in range(SEG_DEV):
        segment = device * SEG_DEV + s
        added = jnp.int32(0)
        user = jnp.int32(0)
        for u in range(USERS):
            hit = ends[u] == segment
            added = jnp.where(hit, news[u], added)
            user = jnp.where(hit, u, user)
        info[s, 0] = lengths[segment]
        info[s, 1] = added
        info[s, 2] = user

    act_user = device * ACT // NEW
    listed = vectors[0][...]
    listing = lax.broadcasted_iota(jnp.int32, listed.shape, 0).astype(F32)
    users = vectors[1][...]
    batch = users.astype(F32)
    for c in range(NC):
        near = device if c == 0 else device + 1 - 2 * core
        for s in range(SEG_DEV):
            hit = listed == near * SEG_DEV + s
            owner = jnp.sum(jnp.where(hit, listing, 0.0), axis=0, keepdims=True)
            owner = jnp.sum(owner, axis=1, keepdims=True)
            k = c * SEG_DEV + s
            marks[k : k + 1] = jnp.where(batch == owner, 1.0, 0.0)
    marks[4:5] = jnp.where(users == act_user, 1.0, 0.0)
    mask[...] = marks[...].astype(BF)

    c, q, a, k, v = weights
    heavy[0].wait()
    heavy[1].wait()
    query = jnp.dot(c[...], q[...], preferred_element_type=F32).astype(BF)
    heavy[2].wait()
    heavy[3].wait()
    key = jnp.dot(a[...], k[...], preferred_element_type=F32)
    heavy[4].wait()
    value = jnp.dot(a[...], v[...], preferred_element_type=F32)
    block[0:2] = key
    block[2:4] = value
    for h in range(HEADS):
        rows[h * 4 : h * 4 + 4] = block[0:4, h * DH : (h + 1) * DH]
    fresh = rows[...].astype(BF)
    for i in range(NZ):
        msg[i, :, 0:W] = query
        msg[i, :, W : W + DH] = fresh
    valid = jnp.clip(news[act_user] - device * ACT % NEW, 0, ACT)
    row = lax.broadcasted_iota(jnp.int32, (ACT, W), 0)
    block[...] = jnp.zeros_like(block)
    block[OWN - ACT : OWN] = key
    own[0] = block[...].astype(BF)
    block[OWN - ACT : OWN] = jnp.where(row < valid, value, 0.0)
    own[1] = block[...].astype(BF)


def project(lists, counts, lengths, news, users, cand, act, wq, wk, wv):
    weight = pltpu.VMEM((D, W), BF)
    return pl.pallas_call(
        project_kernel,
        out_shape=(
            jax.ShapeDtypeStruct((NZ, MB, W + DH), BF),
            jax.ShapeDtypeStruct((2, OWN, W), BF),
            jax.ShapeDtypeStruct((SEG_DEV, 3), jnp.int32),
            jax.ShapeDtypeStruct((8, BATCHES), BF),
        ),
        in_specs=[aspec()] * 10,
        out_specs=(vspec(), vspec(), sspec(), vspec()),
        scratch_shapes=[
            pltpu.SMEM(lists.shape, jnp.int32),
            pltpu.SMEM(counts.shape, jnp.int32),
            pltpu.SMEM(lengths.shape, jnp.int32),
            pltpu.SMEM(news.shape, jnp.int32),
            pltpu.VMEM(lists.shape, jnp.int32),
            pltpu.VMEM((1, BATCHES), jnp.int32),
            pltpu.VMEM((MB, D), BF),
            weight,
            pltpu.VMEM((ACT, D), BF),
            weight,
            weight,
            pltpu.VMEM((MB, DH), F32),
            pltpu.VMEM((OWN, W), F32),
            pltpu.VMEM((8, BATCHES), F32),
            pltpu.SemaphoreType.DMA((11,)),
        ],
        name="project",
    )(lists, counts, lengths, news, users.reshape(1, BATCHES), cand, wq, act, wk, wv)


def stage_kernel(info, own, keys, vals, out):
    rowpos = lax.broadcasted_iota(jnp.int32, (SEG, W), 0)
    for s in range(SEG_DEV):
        lo = s * SEG
        out[lo : lo + SEG] = keys[lo : lo + SEG]
        v = vals[lo : lo + SEG].astype(F32)
        lo += STORED
        out[lo : lo + SEG] = jnp.where(rowpos < info[s, 0], v, 0.0).astype(BF)
    row = lax.broadcasted_iota(jnp.int32, (OWN, W), 0)
    last = keys[SEG - OWN : SEG].astype(F32)
    last = jnp.where(row >= OWN - ACT, own[0].astype(F32), last)
    out[SEG - OWN : SEG] = last.astype(BF)
    out[STORED + SEG - OWN : STORED + SEG] = own[1]


def stage(info, own, keys, vals):
    return pl.pallas_call(
        stage_kernel,
        out_shape=jax.ShapeDtypeStruct((2 * STORED, W), BF),
        in_specs=[sspec()] + [vspec()] * 3,
        out_specs=vspec(),
        compiler_params=params(16),
        cost_estimate=cost(1_000_000, 2_200_000),
        name="stage",
    )(info, own, keys, vals)


def spread_kernel(arr, out):
    rows = arr[...]
    for t in range(NX):
        out[t] = rows


def spread(arr):
    return pl.pallas_call(
        spread_kernel,
        out_shape=jax.ShapeDtypeStruct((NX, ZROWS, W + DH), BF),
        in_specs=[vspec()],
        out_specs=vspec(),
        compiler_params=params(8),
        name="spread",
    )(arr)


def append_kernel(info, arr, keys, vals, new_keys, new_vals):
    s = pl.program_id(0)
    length = info[s, 0]
    added = info[s, 1]
    user = info[s, 2]
    start = ((user * 4 + (NZ - FIRST_Z)) % NZ) * MB
    fresh = arr[:, pl.ds(pl.multiple_of(start, 4 * MB), 4 * MB), :].reshape(XC * 4 * MB, DH)
    shape = (SEG, XC * 4 * MB)
    pos = lax.broadcasted_iota(jnp.int32, shape, 0) - length
    j = lax.broadcasted_iota(jnp.int32, shape, 1)
    source = ((j // 32 + FIRST_X) % NX) * NC + j // 128
    step = ((j // 8) % 4) * 16 + source * 2 + j % 2
    kind = (j // 2) % 4
    rowpos = lax.broadcasted_iota(jnp.int32, (SEG, DH), 0)
    fill = (rowpos >= length) & (rowpos < length + added)
    for h in range(HEADS):
        cs = slice(h * DH, (h + 1) * DH)
        for i, (old, new) in enumerate(((keys, new_keys), (vals, new_vals))):
            hot = ((pos == step) & (kind == 2 * h + i)).astype(F32).astype(BF)
            placed = jnp.dot(hot, fresh, preferred_element_type=F32)
            new[:, cs] = jnp.where(fill, placed, old[:, cs].astype(F32)).astype(BF)


def append(info, arr, keys, vals):
    rows = SEG_DEV * SEG
    block = pl.BlockSpec((SEG, W), lambda s: (s, 0))
    return pl.pallas_call(
        append_kernel,
        grid=(SEG_DEV,),
        out_shape=(jax.ShapeDtypeStruct((rows, W), BF),) * 2,
        in_specs=[sspec(), pl.BlockSpec((XC, ZROWS, DH), lambda s: (0, 0, 0)), block, block],
        out_specs=(block, block),
        compiler_params=params(16),
        cost_estimate=cost(150_000_000, 2_500_000),
        name="append",
    )(info, arr, keys, vals)


def attend_kernel(maskrow, arr, mine, other, part, fresh, theirs, total, sem):
    copy = pltpu.make_async_copy(other, theirs, sem)
    copy.start()
    fresh[...] = arr[:, :, W:]
    shape = (HALF, BATCHES)
    row = lax.broadcasted_iota(jnp.int32, shape, 0)
    lane = lax.broadcasted_iota(jnp.int32, shape, 1)
    step = (row % ZROWS) // MB
    column = (row // ZROWS + FIRST_X) % NX
    batch = ((step + FIRST_Z) % NZ) * XC + column * NC + lax.axis_index("core")
    hot = (lane == batch).astype(F32).astype(BF)
    use = lax.dot_general(
        hot, maskrow[...], (((1,), (1,)), ((), ())), preferred_element_type=F32
    )

    def weigh(logits):
        e = jnp.exp2(logits * (-SCALE * LOG2E))
        return (logits * SCALE) * pl.reciprocal(1.0 + e, approx=True)

    def score(a, b):
        return lax.dot_general(a, b, (((1,), (1,)), ((), ())), preferred_element_type=F32)

    lane = lax.broadcasted_iota(jnp.int32, (HALF, DH), 1)
    marks = []
    for u in range(NC * SEG_DEV):
        seg = jnp.broadcast_to(use[:, u : u + 1], (HALF, DH))
        marks.append((seg, jnp.where(lane >= DH - ACT, use[:, 4:5], seg)))

    def stored(c, src, h):
        cs = slice(h * DH, (h + 1) * DH)
        logits = score(q[:, cs], src[0:STORED, cs])
        parts = []
        for i in range(STORED // DH):
            s = i * DH // SEG
            last = s == 0 and (i + 1) * DH == SEG
            mark = marks[c * SEG_DEV + s][1 if last else 0]
            parts.append((weigh(logits[:, i * DH : (i + 1) * DH]) * mark).astype(BF))
        wt = jnp.concatenate(parts, axis=1)
        return jnp.dot(wt, src[STORED : 2 * STORED, cs], preferred_element_type=F32)

    q = arr[:, :, 0:W].reshape(HALF, W)
    for h in range(HEADS):
        total[:, h * DH : (h + 1) * DH] = stored(0, mine, h)
    copy.wait()
    for h in range(HEADS):
        cs = slice(h * DH, (h + 1) * DH)
        out = (total[:, cs] + stored(1, theirs, h)).astype(BF)
        for x in range(NX):
            part[x, :, cs] = out[x * ZROWS : (x + 1) * ZROWS]


def attend(maskrow, arr, mine, theirs):
    return pl.pallas_call(
        attend_kernel,
        out_shape=(
            jax.ShapeDtypeStruct((NX, ZROWS, W), BF),
            jax.ShapeDtypeStruct((NX, ZROWS, DH), BF),
        ),
        in_specs=[vspec()] * 3 + [aspec()],
        out_specs=(vspec(),) * 2,
        scratch_shapes=[
            pltpu.VMEM((2 * STORED, W), BF),
            pltpu.VMEM((HALF, W), F32),
            pltpu.SemaphoreType.DMA,
        ],
        compiler_params=params(32),
        name="attend",
    )(maskrow, arr, mine, theirs)


def fold_kernel(arr, out):
    out[...] = jnp.sum(arr[...].astype(F32), axis=0).astype(BF)


def fold(arr):
    return pl.pallas_call(
        fold_kernel,
        out_shape=jax.ShapeDtypeStruct((ZROWS, W), BF),
        in_specs=[vspec()],
        out_specs=vspec(),
        compiler_params=params(8),
        name="fold",
    )(arr)


def two_terms(x):
    hi = x.astype(BF)
    lo = (x - hi.astype(F32)).astype(BF)
    return hi, lo


def gate_kernel(cand, wg, wo, gate, base, own):
    first = pl.multiple_of(lax.axis_index("mp") * W, W)
    own[...] = cand[:, pl.ds(first, W)].astype(F32)
    v = jnp.dot(cand[...], wg[...], preferred_element_type=F32)
    g = v / (1.0 + jnp.exp(-v))
    gate[...] = g
    hi, lo = two_terms(g)
    base[...] = jnp.dot(hi, wo[...], preferred_element_type=F32) + jnp.dot(
        lo, wo[...], preferred_element_type=F32
    )


def gate_and_base(cand, wg, wo):
    return pl.pallas_call(
        gate_kernel,
        out_shape=(
            jax.ShapeDtypeStruct((MB, W), F32),
            jax.ShapeDtypeStruct((MB, D), F32),
            jax.ShapeDtypeStruct((MB, W), F32),
        ),
        in_specs=[vspec()] * 3,
        out_specs=(vspec(),) * 3,
        compiler_params=params(8),
        cost_estimate=cost(10_000_000_000, 40_000_000),
        name="gate",
    )(cand, wg, wo)


MSG = 2 * W + 128


def mix_kernel(arr, gate, base, wo, out):
    att = jnp.sum(arr[...].astype(F32).reshape(NZ, MB, W), axis=0)
    mean = jnp.sum(att, axis=1, keepdims=True) * (1.0 / W)
    d = att - mean
    sq = jnp.sum(d * d, axis=1, keepdims=True)
    hi, lo = two_terms(d * gate[...])
    a = jnp.dot(hi, wo[...], preferred_element_type=F32) + jnp.dot(
        lo, wo[...], preferred_element_type=F32
    )
    b = base[...]
    lane = lax.broadcasted_iota(jnp.int32, (MB, 128), 1)
    stats = jnp.where(lane == 0, mean, sq)
    for i in range(MP):
        cs = slice((i + FIRST_Y) % MP * W, ((i + FIRST_Y) % MP + 1) * W)
        out[i, :, 0:W] = a[:, cs]
        out[i, :, W : 2 * W] = b[:, cs]
        out[i, :, 2 * W : MSG] = stats


def mix(arr, gate, base, wo):
    return pl.pallas_call(
        mix_kernel,
        out_shape=jax.ShapeDtypeStruct((MP, MB, MSG), F32),
        in_specs=[vspec()] * 4,
        out_specs=vspec(),
        compiler_params=params(8),
        name="mix",
    )(arr, gate, base, wo)


def finish_kernel(arr, own, out):
    means = [arr[i, :, 2 * W : 2 * W + 1] for i in range(MP)]
    mean = sum(means) * (1.0 / MP)
    square = sum(arr[i, :, 2 * W + 1 : 2 * W + 2] for i in range(MP))
    square = square + W * sum((m - mean) * (m - mean) for m in means)
    scale = lax.rsqrt(square * (1.0 / D) + 1e-05)
    total = sum(
        arr[i, :, 0:W] + (means[i] - mean) * arr[i, :, W : 2 * W] for i in range(MP)
    )
    out[...] = (own[...] + total * scale).astype(BF)


def finish(arr, own):
    return pl.pallas_call(
        finish_kernel,
        out_shape=jax.ShapeDtypeStruct((MB, W), BF),
        in_specs=[vspec()] * 2,
        out_specs=vspec(),
        compiler_params=params(8),
        name="finish",
    )(arr, own)


def exchange(x, axis, size, first):
    groups = [[(i + first) % size for i in range(size)]]
    return lax.all_to_all(
        x, axis, split_axis=0, concat_axis=0, tiled=True, axis_index_groups=groups
    )


def per_device(
    candidates,
    actions,
    hist_keys,
    hist_values,
    w_query,
    w_gate,
    w_key,
    w_value,
    w_out,
    segment_list,
    segment_count,
    segment_length,
    new_count,
    batch_user,
):
    with jax.named_scope("gather"):
        message, own, info, mask = project(
            segment_list,
            segment_count,
            segment_length,
            new_count,
            batch_user,
            candidates,
            actions,
            w_query,
            w_key,
            w_value,
        )
        arrived = exchange(message, "z", NZ, FIRST_Z)
    with jax.named_scope("share"):
        mine = stage(info, own, hist_keys, hist_values)
        theirs = lax.ppermute(mine, "core", [(0, 1), (1, 0)])
        gate, base, residual = gate_and_base(candidates, w_gate, w_out)
        arrived, gate, base, residual = lax.optimization_barrier(
            (arrived, gate, base, residual)
        )
    with jax.named_scope("gather"):
        arrived = exchange(spread(arrived.reshape(ZROWS, W + DH)), "x", NX, FIRST_X)
    with jax.named_scope("attend"):
        part, fresh = attend(mask, arrived, mine, theirs)
    with jax.named_scope("return"):
        part = exchange(part, "x", NX, FIRST_X)
    with jax.named_scope("append"):
        fresh = lax.all_gather(fresh, "core", axis=0).reshape(XC, ZROWS, DH)
        new_keys, new_values = append(info, fresh, hist_keys, hist_values)
    with jax.named_scope("return"):
        part, new_keys, new_values = lax.optimization_barrier((part, new_keys, new_values))
        summed = exchange(fold(part), "z", NZ, FIRST_Z)
    with jax.named_scope("mix"):
        mixed = exchange(mix(summed, gate, base, w_out), "mp", MP, FIRST_Y)
        ranked = finish(mixed, residual)
    return (ranked, new_keys, new_values)


def solution(mesh):
    names = ("z", "x", "core", "mp")
    inner = Mesh(mesh.devices.reshape(NZ, NX, NC, MP), names)
    hist = ("z", "x", "core")
    in_specs = (
        P(hist, None),
        P(hist, None),
        P(hist, "mp"),
        P(hist, "mp"),
        P(None, "mp"),
        P(None, "mp"),
        P(None, "mp"),
        P(None, "mp"),
        P("mp", None),
        P(),
        P(),
        P(),
        P(),
        P(),
    )
    out_specs = (P(hist, "mp"), P(hist, "mp"), P(hist, "mp"))
    return jax.shard_map(
        per_device, mesh=inner, in_specs=in_specs, out_specs=out_specs, check_vma=False
    )
```

```python
import functools
import math

import jax
import jax.numpy as jnp
from jax import lax
from jax.experimental import pallas as pl
from jax.experimental.pallas import tpu as pltpu
from jax.sharding import Mesh
from jax.sharding import PartitionSpec as P

D = 1024
DH = 128
SEG = 512
NEW = 64
USERS = 4
NZ = 16
NX = 4
NC = 2
XC = NX * NC
ZX = NZ * NX
MP = 4
MB = 8
SEG_DEV = 2
W = D // MP
HEADS = W // DH
BATCHES = NZ * XC
QROWS = BATCHES * MB
HALF = ZX * MB
ZROWS = NZ * MB
FIRST_Z = 8
FIRST_X = 2
FIRST_Y = 3
STORED = SEG_DEV * SEG
OWN = 16
PATCH = NEW + 16
HEAD = SEG // 4
ACT = 2
SCALE = 1.0 / math.sqrt(DH)
LOG2E = 1.4426950408889634
BF = jnp.bfloat16
F32 = jnp.float32
MIB = 1024 * 1024


def vspec():
    return pl.BlockSpec(memory_space=pltpu.VMEM)


def sspec():
    return pl.BlockSpec(memory_space=pltpu.SMEM)


def aspec():
    return pl.BlockSpec(memory_space=pl.ANY)


def params(mib):
    return pltpu.CompilerParams(vmem_limit_bytes=mib * MIB)


def cost(flops, nbytes):
    return pl.CostEstimate(flops=flops, bytes_accessed=nbytes, transcendentals=0)


def place():
    core = lax.axis_index("core")
    return core, lax.axis_index("z") * XC + lax.axis_index("x") * NC + core


def project_kernel(*refs):
    small, big, outs = refs[:5], refs[5:10], refs[10:14]
    scalars, vectors, weights = refs[14:18], refs[18:20], refs[20:25]
    rows, block, marks, sems = refs[25:]
    msg, own, info, mask = outs
    heavy = [pltpu.make_async_copy(x, y, sems.at[i]) for i, (x, y) in enumerate(zip(big, weights))]
    sources = small[:4] + (small[0], small[4])
    light = [
        pltpu.make_async_copy(x, y, sems.at[5 + i])
        for i, (x, y) in enumerate(zip(sources, scalars + vectors))
    ]
    for copy in heavy[:2] + light + heavy[2:]:
        copy.start()
    block[...] = jnp.zeros_like(block)
    marks[...] = jnp.zeros_like(marks)
    for copy in light:
        copy.wait()

    lists, counts, lengths, news = scalars
    core, device = place()
    ends = [lists[u, counts[u] - 1] for u in range(USERS)]
    for s in range(SEG_DEV):
        segment = device * SEG_DEV + s
        added = jnp.int32(0)
        user = jnp.int32(0)
        for u in range(USERS):
            hit = ends[u] == segment
            added = jnp.where(hit, news[u], added)
            user = jnp.where(hit, u, user)
        info[s, 0] = lengths[segment]
        info[s, 1] = added
        info[s, 2] = user

    act_user = device * ACT // NEW
    listed = vectors[0][...]
    listing = lax.broadcasted_iota(jnp.int32, listed.shape, 0).astype(F32)
    users = vectors[1][...]
    batch = users.astype(F32)
    for c in range(NC):
        near = device if c == 0 else device + 1 - 2 * core
        for s in range(SEG_DEV):
            hit = listed == near * SEG_DEV + s
            owner = jnp.sum(jnp.where(hit, listing, 0.0), axis=0, keepdims=True)
            owner = jnp.sum(owner, axis=1, keepdims=True)
            k = c * SEG_DEV + s
            marks[k : k + 1] = jnp.where(batch == owner, 1.0, 0.0)
    marks[4:5] = jnp.where(users == act_user, 1.0, 0.0)
    mask[...] = marks[...].astype(BF)

    c, q, a, k, v = weights
    heavy[0].wait()
    heavy[1].wait()
    query = jnp.dot(c[...], q[...], preferred_element_type=F32).astype(BF)
    heavy[2].wait()
    heavy[3].wait()
    key = jnp.dot(a[...], k[...], preferred_element_type=F32)
    heavy[4].wait()
    value = jnp.dot(a[...], v[...], preferred_element_type=F32)
    block[0:2] = key
    block[2:4] = value
    for h in range(HEADS):
        rows[h * 4 : h * 4 + 4] = block[0:4, h * DH : (h + 1) * DH]
    fresh = rows[...].astype(BF)
    for i in range(NZ):
        msg[i, :, 0:W] = query
        msg[i, :, W : W + DH] = fresh
    valid = jnp.clip(news[act_user] - device * ACT % NEW, 0, ACT)
    row = lax.broadcasted_iota(jnp.int32, (ACT, W), 0)
    block[...] = jnp.zeros_like(block)
    block[OWN - ACT : OWN] = key
    own[0] = block[...].astype(BF)
    block[OWN - ACT : OWN] = jnp.where(row < valid, value, 0.0)
    own[1] = block[...].astype(BF)


def project(lists, counts, lengths, news, users, cand, act, wq, wk, wv):
    weight = pltpu.VMEM((D, W), BF)
    return pl.pallas_call(
        project_kernel,
        out_shape=(
            jax.ShapeDtypeStruct((NZ, MB, W + DH), BF),
            jax.ShapeDtypeStruct((2, OWN, W), BF),
            jax.ShapeDtypeStruct((SEG_DEV, 3), jnp.int32),
            jax.ShapeDtypeStruct((8, BATCHES), BF),
        ),
        in_specs=[aspec()] * 10,
        out_specs=(vspec(), vspec(), sspec(), vspec()),
        scratch_shapes=[
            pltpu.SMEM(lists.shape, jnp.int32),
            pltpu.SMEM(counts.shape, jnp.int32),
            pltpu.SMEM(lengths.shape, jnp.int32),
            pltpu.SMEM(news.shape, jnp.int32),
            pltpu.VMEM(lists.shape, jnp.int32),
            pltpu.VMEM((1, BATCHES), jnp.int32),
            pltpu.VMEM((MB, D), BF),
            weight,
            pltpu.VMEM((ACT, D), BF),
            weight,
            weight,
            pltpu.VMEM((MB, DH), F32),
            pltpu.VMEM((OWN, W), F32),
            pltpu.VMEM((8, BATCHES), F32),
            pltpu.SemaphoreType.DMA((11,)),
        ],
        name="project",
    )(lists, counts, lengths, news, users.reshape(1, BATCHES), cand, wq, act, wk, wv)


def stage_kernel(info, own, keys, vals, out):
    rowpos = lax.broadcasted_iota(jnp.int32, (SEG, W), 0)
    for s in range(SEG_DEV):
        lo = s * SEG
        out[lo : lo + SEG] = keys[lo : lo + SEG]
        v = vals[lo : lo + SEG].astype(F32)
        lo += STORED
        out[lo : lo + SEG] = jnp.where(rowpos < info[s, 0], v, 0.0).astype(BF)
    row = lax.broadcasted_iota(jnp.int32, (OWN, W), 0)
    last = keys[SEG - OWN : SEG].astype(F32)
    last = jnp.where(row >= OWN - ACT, own[0].astype(F32), last)
    out[SEG - OWN : SEG] = last.astype(BF)
    out[STORED + SEG - OWN : STORED + SEG] = own[1]


def stage(info, own, keys, vals):
    return pl.pallas_call(
        stage_kernel,
        out_shape=jax.ShapeDtypeStruct((2 * STORED, W), BF),
        in_specs=[sspec()] + [vspec()] * 3,
        out_specs=vspec(),
        compiler_params=params(16),
        cost_estimate=cost(1_000_000, 2_200_000),
        name="stage",
    )(info, own, keys, vals)


def spread_kernel(arr, out):
    rows = arr[...]
    for t in range(NX):
        out[t] = rows


def spread(arr):
    return pl.pallas_call(
        spread_kernel,
        out_shape=jax.ShapeDtypeStruct((NX, ZROWS, W + DH), BF),
        in_specs=[vspec()],
        out_specs=vspec(),
        compiler_params=params(8),
        name="spread",
    )(arr)


def append_kernel(info, arr, keys, vals, new_keys, new_vals, patch, sems):
    pairs = ((keys, new_keys), (vals, new_vals))
    copies = []
    for s in range(SEG_DEV):
        rows = pl.ds(s * SEG, HEAD)
        for i, (old, new) in enumerate(pairs):
            copies.append(
                pltpu.make_async_copy(old.at[rows], new.at[rows], sems.at[s * 2 + i])
            )
            copies[-1].start()

    shape = (PATCH, XC * 4 * MB)
    j = lax.broadcasted_iota(jnp.int32, shape, 1)
    source = ((j // 32 + FIRST_X) % NX) * NC + j // 128
    step = ((j // 8) % 4) * 16 + source * 2 + j % 2
    kind = (j // 2) % 4
    for s in range(SEG_DEV):
        length = info[s, 0]
        begin = jnp.clip((length // 16) * 16, HEAD, SEG - PATCH)
        rows = pl.ds(pl.multiple_of(s * SEG + begin, 16), PATCH)
        inner = pl.ds(pl.multiple_of(begin - HEAD, 16), PATCH)
        tail = pl.ds(s * SEG + HEAD, SEG - HEAD)
        start = ((info[s, 2] * 4 + (NZ - FIRST_Z)) % NZ) * MB
        fresh = arr[:, pl.ds(pl.multiple_of(start, 4 * MB), 4 * MB), :]
        fresh = fresh.reshape(XC * 4 * MB, DH)
        match = lax.broadcasted_iota(jnp.int32, shape, 0) + (begin - length) == step
        rowpos = lax.broadcasted_iota(jnp.int32, (PATCH, DH), 0) + (begin - length)
        fill = (rowpos >= 0) & (rowpos < info[s, 1])
        for i, (old, new) in enumerate(pairs):
            slot = s * 2 + i
            patch[slot] = old[tail]
            for h in range(HEADS):
                cs = slice(h * DH, (h + 1) * DH)
                hot = (match & (kind == 2 * h + i)).astype(F32).astype(BF)
                placed = jnp.dot(hot, fresh, preferred_element_type=F32)
                kept = old[rows, cs].astype(F32)
                patch[slot, inner, cs] = jnp.where(fill, placed, kept).astype(BF)
            copies.append(
                pltpu.make_async_copy(patch.at[slot], new.at[tail], sems.at[4 + slot])
            )
            copies[-1].start()
    for copy in copies:
        copy.wait()


def append(info, arr, keys, vals):
    stored = jax.ShapeDtypeStruct((STORED, W), BF)
    return pl.pallas_call(
        append_kernel,
        out_shape=(stored,) * 2,
        in_specs=[sspec()] + [vspec()] * 3,
        out_specs=(aspec(),) * 2,
        scratch_shapes=[
            pltpu.VMEM((SEG_DEV * 2, SEG - HEAD, W), BF),
            pltpu.SemaphoreType.DMA((SEG_DEV * 4,)),
        ],
        compiler_params=params(16),
        cost_estimate=cost(150_000_000, 2_500_000),
        name="append",
    )(info, arr, keys, vals)


def attend_kernel(maskrow, arr, mine, other, part, fresh, theirs, total, sem):
    copy = pltpu.make_async_copy(other, theirs, sem)
    copy.start()
    fresh[...] = arr[:, :, W:]
    shape = (HALF, BATCHES)
    row = lax.broadcasted_iota(jnp.int32, shape, 0)
    lane = lax.broadcasted_iota(jnp.int32, shape, 1)
    step = (row % ZROWS) // MB
    column = (row // ZROWS + FIRST_X) % NX
    batch = ((step + FIRST_Z) % NZ) * XC + column * NC + lax.axis_index("core")
    hot = (lane == batch).astype(F32).astype(BF)
    use = lax.dot_general(
        hot, maskrow[...], (((1,), (1,)), ((), ())), preferred_element_type=F32
    )

    def weigh(logits):
        e = jnp.exp2(logits * (-SCALE * LOG2E))
        return (logits * SCALE) * pl.reciprocal(1.0 + e, approx=True)

    def score(a, b):
        return lax.dot_general(a, b, (((1,), (1,)), ((), ())), preferred_element_type=F32)

    lane = lax.broadcasted_iota(jnp.int32, (HALF, DH), 1)
    marks = []
    for u in range(NC * SEG_DEV):
        seg = jnp.broadcast_to(use[:, u : u + 1], (HALF, DH))
        edge = jnp.where(lane >= DH - ACT, use[:, 4:5], seg)
        marks.append((seg.astype(BF), edge.astype(BF)))

    def stored(c, src, h):
        cs = slice(h * DH, (h + 1) * DH)
        logits = score(q[:, cs], src[0:STORED, cs])
        parts = []
        for i in range(STORED // DH):
            s = i * DH // SEG
            last = s == 0 and (i + 1) * DH == SEG
            mark = marks[c * SEG_DEV + s][1 if last else 0]
            parts.append(weigh(logits[:, i * DH : (i + 1) * DH]).astype(BF) * mark)
        wt = jnp.concatenate(parts, axis=1)
        return jnp.dot(wt, src[STORED : 2 * STORED, cs], preferred_element_type=F32)

    q = arr[:, :, 0:W].reshape(HALF, W)
    for h in range(HEADS):
        total[:, h * DH : (h + 1) * DH] = stored(0, mine, h)
    copy.wait()
    for h in range(HEADS):
        cs = slice(h * DH, (h + 1) * DH)
        out = (total[:, cs] + stored(1, theirs, h)).astype(BF)
        for x in range(NX):
            part[x, :, cs] = out[x * ZROWS : (x + 1) * ZROWS]


def attend(maskrow, arr, mine, theirs):
    return pl.pallas_call(
        attend_kernel,
        out_shape=(
            jax.ShapeDtypeStruct((NX, ZROWS, W), BF),
            jax.ShapeDtypeStruct((NX, ZROWS, DH), BF),
        ),
        in_specs=[vspec()] * 3 + [aspec()],
        out_specs=(vspec(),) * 2,
        scratch_shapes=[
            pltpu.VMEM((2 * STORED, W), BF),
            pltpu.VMEM((HALF, W), F32),
            pltpu.SemaphoreType.DMA,
        ],
        compiler_params=params(32),
        name="attend",
    )(maskrow, arr, mine, theirs)


def fold_kernel(arr, out):
    out[...] = jnp.sum(arr[...].astype(F32), axis=0).astype(BF)


def fold(arr):
    return pl.pallas_call(
        fold_kernel,
        out_shape=jax.ShapeDtypeStruct((ZROWS, W), BF),
        in_specs=[vspec()],
        out_specs=vspec(),
        compiler_params=params(8),
        name="fold",
    )(arr)


def two_terms(x):
    hi = x.astype(BF)
    lo = (x - hi.astype(F32)).astype(BF)
    return hi, lo


def gate_kernel(cand, wg, wo, gate, base, own):
    first = pl.multiple_of(lax.axis_index("mp") * W, W)
    own[...] = cand[:, pl.ds(first, W)].astype(F32)
    v = jnp.dot(cand[...], wg[...], preferred_element_type=F32)
    g = v / (1.0 + jnp.exp(-v))
    gate[...] = g
    hi, lo = two_terms(g)
    base[...] = jnp.dot(hi, wo[...], preferred_element_type=F32) + jnp.dot(
        lo, wo[...], preferred_element_type=F32
    )


def gate_and_base(cand, wg, wo):
    return pl.pallas_call(
        gate_kernel,
        out_shape=(
            jax.ShapeDtypeStruct((MB, W), F32),
            jax.ShapeDtypeStruct((MB, D), F32),
            jax.ShapeDtypeStruct((MB, W), F32),
        ),
        in_specs=[vspec()] * 3,
        out_specs=(vspec(),) * 3,
        compiler_params=params(8),
        cost_estimate=cost(10_000_000_000, 40_000_000),
        name="gate",
    )(cand, wg, wo)


MSG = 2 * W + 128


def mix_kernel(arr, gate, base, wo, out):
    att = jnp.sum(arr[...].astype(F32).reshape(NZ, MB, W), axis=0)
    mean = jnp.sum(att, axis=1, keepdims=True) * (1.0 / W)
    d = att - mean
    sq = jnp.sum(d * d, axis=1, keepdims=True)
    hi, lo = two_terms(d * gate[...])
    a = jnp.dot(hi, wo[...], preferred_element_type=F32) + jnp.dot(
        lo, wo[...], preferred_element_type=F32
    )
    b = base[...]
    lane = lax.broadcasted_iota(jnp.int32, (MB, 128), 1)
    stats = jnp.where(lane == 0, mean, sq)
    for i in range(MP):
        cs = slice((i + FIRST_Y) % MP * W, ((i + FIRST_Y) % MP + 1) * W)
        out[i, :, 0:W] = a[:, cs]
        out[i, :, W : 2 * W] = b[:, cs]
        out[i, :, 2 * W : MSG] = stats


def mix(arr, gate, base, wo):
    return pl.pallas_call(
        mix_kernel,
        out_shape=jax.ShapeDtypeStruct((MP, MB, MSG), F32),
        in_specs=[vspec()] * 4,
        out_specs=vspec(),
        compiler_params=params(8),
        name="mix",
    )(arr, gate, base, wo)


def finish_kernel(arr, own, out):
    means = [arr[i, :, 2 * W : 2 * W + 1] for i in range(MP)]
    mean = sum(means) * (1.0 / MP)
    square = sum(arr[i, :, 2 * W + 1 : 2 * W + 2] for i in range(MP))
    square = square + W * sum((m - mean) * (m - mean) for m in means)
    scale = lax.rsqrt(square * (1.0 / D) + 1e-05)
    total = sum(
        arr[i, :, 0:W] + (means[i] - mean) * arr[i, :, W : 2 * W] for i in range(MP)
    )
    out[...] = (own[...] + total * scale).astype(BF)


def finish(arr, own):
    return pl.pallas_call(
        finish_kernel,
        out_shape=jax.ShapeDtypeStruct((MB, W), BF),
        in_specs=[vspec()] * 2,
        out_specs=vspec(),
        compiler_params=params(8),
        name="finish",
    )(arr, own)


def exchange(x, axis, size, first):
    groups = [[(i + first) % size for i in range(size)]]
    return lax.all_to_all(
        x, axis, split_axis=0, concat_axis=0, tiled=True, axis_index_groups=groups
    )


def per_device(
    candidates,
    actions,
    hist_keys,
    hist_values,
    w_query,
    w_gate,
    w_key,
    w_value,
    w_out,
    segment_list,
    segment_count,
    segment_length,
    new_count,
    batch_user,
):
    with jax.named_scope("gather"):
        message, own, info, mask = project(
            segment_list,
            segment_count,
            segment_length,
            new_count,
            batch_user,
            candidates,
            actions,
            w_query,
            w_key,
            w_value,
        )
        arrived = exchange(message, "z", NZ, FIRST_Z)
    with jax.named_scope("share"):
        mine = stage(info, own, hist_keys, hist_values)
        theirs = lax.ppermute(mine, "core", [(0, 1), (1, 0)])
        gate, base, residual = gate_and_base(candidates, w_gate, w_out)
        arrived, gate, base, residual = lax.optimization_barrier(
            (arrived, gate, base, residual)
        )
    with jax.named_scope("gather"):
        arrived = exchange(spread(arrived.reshape(ZROWS, W + DH)), "x", NX, FIRST_X)
    with jax.named_scope("attend"):
        part, fresh = attend(mask, arrived, mine, theirs)
    with jax.named_scope("return"):
        part = exchange(part, "x", NX, FIRST_X)
    with jax.named_scope("append"):
        fresh = lax.all_gather(fresh, "core", axis=0).reshape(XC, ZROWS, DH)
        new_keys, new_values = append(info, fresh, hist_keys, hist_values)
    with jax.named_scope("return"):
        part, new_keys, new_values = lax.optimization_barrier((part, new_keys, new_values))
        summed = exchange(fold(part), "z", NZ, FIRST_Z)
    with jax.named_scope("mix"):
        mixed = exchange(mix(summed, gate, base, w_out), "mp", MP, FIRST_Y)
        ranked = finish(mixed, residual)
    return (ranked, new_keys, new_values)


def solution(mesh):
    names = ("z", "x", "core", "mp")
    inner = Mesh(mesh.devices.reshape(NZ, NX, NC, MP), names)
    hist = ("z", "x", "core")
    in_specs = (
        P(hist, None),
        P(hist, None),
        P(hist, "mp"),
        P(hist, "mp"),
        P(None, "mp"),
        P(None, "mp"),
        P(None, "mp"),
        P(None, "mp"),
        P("mp", None),
        P(),
        P(),
        P(),
        P(),
        P(),
    )
    out_specs = (P(hist, "mp"), P(hist, "mp"), P(hist, "mp"))
    return jax.shard_map(
        per_device, mesh=inner, in_specs=in_specs, out_specs=out_specs, check_vma=False
    )
```

```python
import functools
import math

import jax
import jax.numpy as jnp
from jax import lax
from jax.experimental import pallas as pl
from jax.experimental.pallas import tpu as pltpu
from jax.sharding import Mesh
from jax.sharding import PartitionSpec as P

D = 1024
DH = 128
SEG = 512
NEW = 64
USERS = 4
NZ = 16
NX = 4
NC = 2
XC = NX * NC
ZX = NZ * NX
MP = 4
MB = 8
SEG_DEV = 2
W = D // MP
HEADS = W // DH
BATCHES = NZ * XC
QROWS = BATCHES * MB
HALF = ZX * MB
ZROWS = NZ * MB
FIRST_Z = 8
FIRST_X = 2
FIRST_Y = 3
STORED = SEG_DEV * SEG
OWN = 16
PATCH = NEW + 16
HEAD = SEG // 4
ACT = 2
SCALE = 1.0 / math.sqrt(DH)
LOG2E = 1.4426950408889634
BF = jnp.bfloat16
F32 = jnp.float32
MIB = 1024 * 1024


def vspec():
    return pl.BlockSpec(memory_space=pltpu.VMEM)


def sspec():
    return pl.BlockSpec(memory_space=pltpu.SMEM)


def aspec():
    return pl.BlockSpec(memory_space=pl.ANY)


def params(mib):
    return pltpu.CompilerParams(vmem_limit_bytes=mib * MIB)


def cost(flops, nbytes):
    return pl.CostEstimate(flops=flops, bytes_accessed=nbytes, transcendentals=0)


def place():
    core = lax.axis_index("core")
    return core, lax.axis_index("z") * XC + lax.axis_index("x") * NC + core


def project_kernel(*refs):
    small, big, outs = refs[:5], refs[5:10], refs[10:14]
    scalars, vectors, weights = refs[14:18], refs[18:20], refs[20:23]
    rows, block, marks, sems = refs[23:]
    msg, own, info, mask = outs
    cand, act = big[:2]
    heavy = [
        pltpu.make_async_copy(x, y, sems.at[i])
        for i, (x, y) in enumerate(zip(big[2:], weights))
    ]
    sources = small[:4] + (small[0], small[4])
    light = [
        pltpu.make_async_copy(x, y, sems.at[3 + i])
        for i, (x, y) in enumerate(zip(sources, scalars + vectors))
    ]
    for copy in heavy[:1] + light + heavy[1:]:
        copy.start()
    block[...] = jnp.zeros_like(block)
    marks[...] = jnp.zeros_like(marks)
    for copy in light:
        copy.wait()

    lists, counts, lengths, news = scalars
    core, device = place()
    ends = [lists[u, counts[u] - 1] for u in range(USERS)]
    for s in range(SEG_DEV):
        segment = device * SEG_DEV + s
        added = jnp.int32(0)
        user = jnp.int32(0)
        for u in range(USERS):
            hit = ends[u] == segment
            added = jnp.where(hit, news[u], added)
            user = jnp.where(hit, u, user)
        info[s, 0] = lengths[segment]
        info[s, 1] = added
        info[s, 2] = user

    act_user = device * ACT // NEW
    listed = vectors[0][...]
    listing = lax.broadcasted_iota(jnp.int32, listed.shape, 0).astype(F32)
    users = vectors[1][...]
    batch = users.astype(F32)
    for c in range(NC):
        near = device if c == 0 else device + 1 - 2 * core
        for s in range(SEG_DEV):
            hit = listed == near * SEG_DEV + s
            owner = jnp.sum(jnp.where(hit, listing, 0.0), axis=0, keepdims=True)
            owner = jnp.sum(owner, axis=1, keepdims=True)
            k = c * SEG_DEV + s
            marks[k : k + 1] = jnp.where(batch == owner, 1.0, 0.0)
    marks[4:5] = jnp.where(users == act_user, 1.0, 0.0)
    mask[...] = marks[...].astype(BF)

    q, k, v = weights
    heavy[0].wait()
    query = jnp.dot(cand[...], q[...], preferred_element_type=F32).astype(BF)
    heavy[1].wait()
    key = jnp.dot(act[...], k[...], preferred_element_type=F32)
    heavy[2].wait()
    value = jnp.dot(act[...], v[...], preferred_element_type=F32)
    block[0:2] = key
    block[2:4] = value
    for h in range(HEADS):
        rows[h * 4 : h * 4 + 4] = block[0:4, h * DH : (h + 1) * DH]
    fresh = rows[...].astype(BF)
    for i in range(NZ):
        msg[i, :, 0:W] = query
        msg[i, :, W : W + DH] = fresh
    valid = jnp.clip(news[act_user] - device * ACT % NEW, 0, ACT)
    row = lax.broadcasted_iota(jnp.int32, (ACT, W), 0)
    block[...] = jnp.zeros_like(block)
    block[OWN - ACT : OWN] = key
    own[0] = block[...].astype(BF)
    block[OWN - ACT : OWN] = jnp.where(row < valid, value, 0.0)
    own[1] = block[...].astype(BF)


def project(lists, counts, lengths, news, users, cand, act, wq, wk, wv):
    weight = pltpu.VMEM((D, W), BF)
    return pl.pallas_call(
        project_kernel,
        out_shape=(
            jax.ShapeDtypeStruct((NZ, MB, W + DH), BF),
            jax.ShapeDtypeStruct((2, OWN, W), BF),
            jax.ShapeDtypeStruct((SEG_DEV, 3), jnp.int32),
            jax.ShapeDtypeStruct((8, BATCHES), BF),
        ),
        in_specs=[aspec()] * 5 + [vspec()] * 2 + [aspec()] * 3,
        out_specs=(vspec(), vspec(), sspec(), vspec()),
        scratch_shapes=[
            pltpu.SMEM(lists.shape, jnp.int32),
            pltpu.SMEM(counts.shape, jnp.int32),
            pltpu.SMEM(lengths.shape, jnp.int32),
            pltpu.SMEM(news.shape, jnp.int32),
            pltpu.VMEM(lists.shape, jnp.int32),
            pltpu.VMEM((1, BATCHES), jnp.int32),
            weight,
            weight,
            weight,
            pltpu.VMEM((MB, DH), F32),
            pltpu.VMEM((OWN, W), F32),
            pltpu.VMEM((8, BATCHES), F32),
            pltpu.SemaphoreType.DMA((9,)),
        ],
        name="project",
    )(lists, counts, lengths, news, users.reshape(1, BATCHES), cand, act, wq, wk, wv)


def stage_kernel(info, own, keys, vals, out):
    rowpos = lax.broadcasted_iota(jnp.int32, (SEG, W), 0)
    for s in range(SEG_DEV):
        lo = s * SEG
        out[lo : lo + SEG] = keys[lo : lo + SEG]
        v = vals[lo : lo + SEG].astype(F32)
        lo += STORED
        out[lo : lo + SEG] = jnp.where(rowpos < info[s, 0], v, 0.0).astype(BF)
    row = lax.broadcasted_iota(jnp.int32, (OWN, W), 0)
    last = keys[SEG - OWN : SEG].astype(F32)
    last = jnp.where(row >= OWN - ACT, own[0].astype(F32), last)
    out[SEG - OWN : SEG] = last.astype(BF)
    out[STORED + SEG - OWN : STORED + SEG] = own[1]


def stage(info, own, keys, vals):
    return pl.pallas_call(
        stage_kernel,
        out_shape=jax.ShapeDtypeStruct((2 * STORED, W), BF),
        in_specs=[sspec()] + [vspec()] * 3,
        out_specs=vspec(),
        compiler_params=params(16),
        cost_estimate=cost(1_000_000, 2_200_000),
        name="stage",
    )(info, own, keys, vals)


def spread_kernel(arr, out):
    rows = arr[...]
    for t in range(NX):
        out[t] = rows


def spread(arr):
    return pl.pallas_call(
        spread_kernel,
        out_shape=jax.ShapeDtypeStruct((NX, ZROWS, W + DH), BF),
        in_specs=[vspec()],
        out_specs=vspec(),
        compiler_params=params(8),
        name="spread",
    )(arr)


def append_kernel(info, arr, keys, vals, new_keys, new_vals, patch, sems):
    pairs = ((keys, new_keys), (vals, new_vals))
    copies = []
    for s in range(SEG_DEV):
        rows = pl.ds(s * SEG, HEAD)
        for i, (old, new) in enumerate(pairs):
            copies.append(
                pltpu.make_async_copy(old.at[rows], new.at[rows], sems.at[s * 2 + i])
            )
            copies[-1].start()

    shape = (PATCH, XC * 4 * MB)
    j = lax.broadcasted_iota(jnp.int32, shape, 1)
    source = ((j // 32 + FIRST_X) % NX) * NC + j // 128
    step = ((j // 8) % 4) * 16 + source * 2 + j % 2
    kind = (j // 2) % 4
    for s in range(SEG_DEV):
        length = info[s, 0]
        begin = jnp.clip((length // 16) * 16, HEAD, SEG - PATCH)
        rows = pl.ds(pl.multiple_of(s * SEG + begin, 16), PATCH)
        inner = pl.ds(pl.multiple_of(begin - HEAD, 16), PATCH)
        tail = pl.ds(s * SEG + HEAD, SEG - HEAD)
        start = ((info[s, 2] * 4 + (NZ - FIRST_Z)) % NZ) * MB
        fresh = arr[:, pl.ds(pl.multiple_of(start, 4 * MB), 4 * MB), :]
        fresh = fresh.reshape(XC * 4 * MB, DH)
        match = lax.broadcasted_iota(jnp.int32, shape, 0) + (begin - length) == step
        rowpos = lax.broadcasted_iota(jnp.int32, (PATCH, DH), 0) + (begin - length)
        fill = (rowpos >= 0) & (rowpos < info[s, 1])
        for i, (old, new) in enumerate(pairs):
            slot = s * 2 + i
            patch[slot] = old[tail]
            for h in range(HEADS):
                cs = slice(h * DH, (h + 1) * DH)
                hot = (match & (kind == 2 * h + i)).astype(F32).astype(BF)
                placed = jnp.dot(hot, fresh, preferred_element_type=F32)
                kept = old[rows, cs].astype(F32)
                patch[slot, inner, cs] = jnp.where(fill, placed, kept).astype(BF)
            copies.append(
                pltpu.make_async_copy(patch.at[slot], new.at[tail], sems.at[4 + slot])
            )
            copies[-1].start()
    for copy in copies:
        copy.wait()


def append(info, arr, keys, vals):
    stored = jax.ShapeDtypeStruct((STORED, W), BF)
    return pl.pallas_call(
        append_kernel,
        out_shape=(stored,) * 2,
        in_specs=[sspec()] + [vspec()] * 3,
        out_specs=(aspec(),) * 2,
        scratch_shapes=[
            pltpu.VMEM((SEG_DEV * 2, SEG - HEAD, W), BF),
            pltpu.SemaphoreType.DMA((SEG_DEV * 4,)),
        ],
        compiler_params=params(16),
        cost_estimate=cost(150_000_000, 2_500_000),
        name="append",
    )(info, arr, keys, vals)


def attend_kernel(maskrow, arr, mine, other, part, fresh, theirs, total, sem):
    copy = pltpu.make_async_copy(other, theirs, sem)
    copy.start()
    fresh[...] = arr[:, :, W:]
    shape = (HALF, BATCHES)
    row = lax.broadcasted_iota(jnp.int32, shape, 0)
    lane = lax.broadcasted_iota(jnp.int32, shape, 1)
    step = (row % ZROWS) // MB
    column = (row // ZROWS + FIRST_X) % NX
    batch = ((step + FIRST_Z) % NZ) * XC + column * NC + lax.axis_index("core")
    hot = (lane == batch).astype(F32).astype(BF)
    use = lax.dot_general(
        hot, maskrow[...], (((1,), (1,)), ((), ())), preferred_element_type=F32
    )

    def weigh(logits):
        e = jnp.exp2(logits * (-SCALE * LOG2E))
        return (logits * SCALE) * pl.reciprocal(1.0 + e, approx=True)

    def score(a, b):
        return lax.dot_general(a, b, (((1,), (1,)), ((), ())), preferred_element_type=F32)

    lane = lax.broadcasted_iota(jnp.int32, (HALF, DH), 1)
    marks = []
    for u in range(NC * SEG_DEV):
        seg = jnp.broadcast_to(use[:, u : u + 1], (HALF, DH))
        edge = jnp.where(lane >= DH - ACT, use[:, 4:5], seg)
        marks.append((seg.astype(BF), edge.astype(BF)))

    def stored(c, src, h):
        cs = slice(h * DH, (h + 1) * DH)
        logits = score(q[:, cs], src[0:STORED, cs])
        parts = []
        for i in range(STORED // DH):
            s = i * DH // SEG
            last = s == 0 and (i + 1) * DH == SEG
            mark = marks[c * SEG_DEV + s][1 if last else 0]
            parts.append(weigh(logits[:, i * DH : (i + 1) * DH]).astype(BF) * mark)
        wt = jnp.concatenate(parts, axis=1)
        return jnp.dot(wt, src[STORED : 2 * STORED, cs], preferred_element_type=F32)

    q = arr[:, :, 0:W].reshape(HALF, W)
    for h in range(HEADS):
        total[:, h * DH : (h + 1) * DH] = stored(0, mine, h)
    copy.wait()
    for h in range(HEADS):
        cs = slice(h * DH, (h + 1) * DH)
        out = (total[:, cs] + stored(1, theirs, h)).astype(BF)
        for x in range(NX):
            part[x, :, cs] = out[x * ZROWS : (x + 1) * ZROWS]


def attend(maskrow, arr, mine, theirs):
    return pl.pallas_call(
        attend_kernel,
        out_shape=(
            jax.ShapeDtypeStruct((NX, ZROWS, W), BF),
            jax.ShapeDtypeStruct((NX, ZROWS, DH), BF),
        ),
        in_specs=[vspec()] * 3 + [aspec()],
        out_specs=(vspec(),) * 2,
        scratch_shapes=[
            pltpu.VMEM((2 * STORED, W), BF),
            pltpu.VMEM((HALF, W), F32),
            pltpu.SemaphoreType.DMA,
        ],
        compiler_params=params(32),
        name="attend",
    )(maskrow, arr, mine, theirs)


def fold_kernel(arr, out):
    out[...] = jnp.sum(arr[...].astype(F32), axis=0).astype(BF)


def fold(arr):
    return pl.pallas_call(
        fold_kernel,
        out_shape=jax.ShapeDtypeStruct((ZROWS, W), BF),
        in_specs=[vspec()],
        out_specs=vspec(),
        compiler_params=params(8),
        name="fold",
    )(arr)


def two_terms(x):
    hi = x.astype(BF)
    lo = (x - hi.astype(F32)).astype(BF)
    return hi, lo


def gate_kernel(cand, wg, wo, gate, base, own):
    first = pl.multiple_of(lax.axis_index("mp") * W, W)
    own[...] = cand[:, pl.ds(first, W)].astype(F32)
    v = jnp.dot(cand[...], wg[...], preferred_element_type=F32)
    g = v / (1.0 + jnp.exp(-v))
    gate[...] = g
    hi, lo = two_terms(g)
    base[...] = jnp.dot(hi, wo[...], preferred_element_type=F32) + jnp.dot(
        lo, wo[...], preferred_element_type=F32
    )


def gate_and_base(cand, wg, wo):
    return pl.pallas_call(
        gate_kernel,
        out_shape=(
            jax.ShapeDtypeStruct((MB, W), F32),
            jax.ShapeDtypeStruct((MB, D), F32),
            jax.ShapeDtypeStruct((MB, W), F32),
        ),
        in_specs=[vspec()] * 3,
        out_specs=(vspec(),) * 3,
        compiler_params=params(8),
        cost_estimate=cost(10_000_000_000, 40_000_000),
        name="gate",
    )(cand, wg, wo)


MSG = 2 * W + 128


def mix_kernel(arr, gate, base, wo, out):
    att = jnp.sum(arr[...].astype(F32).reshape(NZ, MB, W), axis=0)
    mean = jnp.sum(att, axis=1, keepdims=True) * (1.0 / W)
    d = att - mean
    sq = jnp.sum(d * d, axis=1, keepdims=True)
    hi, lo = two_terms(d * gate[...])
    a = jnp.dot(hi, wo[...], preferred_element_type=F32) + jnp.dot(
        lo, wo[...], preferred_element_type=F32
    )
    b = base[...]
    lane = lax.broadcasted_iota(jnp.int32, (MB, 128), 1)
    stats = jnp.where(lane == 0, mean, sq)
    for i in range(MP):
        cs = slice((i + FIRST_Y) % MP * W, ((i + FIRST_Y) % MP + 1) * W)
        out[i, :, 0:W] = a[:, cs]
        out[i, :, W : 2 * W] = b[:, cs]
        out[i, :, 2 * W : MSG] = stats


def mix(arr, gate, base, wo):
    return pl.pallas_call(
        mix_kernel,
        out_shape=jax.ShapeDtypeStruct((MP, MB, MSG), F32),
        in_specs=[vspec()] * 4,
        out_specs=vspec(),
        compiler_params=params(8),
        name="mix",
    )(arr, gate, base, wo)


def finish_kernel(arr, own, out):
    means = [arr[i, :, 2 * W : 2 * W + 1] for i in range(MP)]
    mean = sum(means) * (1.0 / MP)
    square = sum(arr[i, :, 2 * W + 1 : 2 * W + 2] for i in range(MP))
    square = square + W * sum((m - mean) * (m - mean) for m in means)
    scale = lax.rsqrt(square * (1.0 / D) + 1e-05)
    total = sum(
        arr[i, :, 0:W] + (means[i] - mean) * arr[i, :, W : 2 * W] for i in range(MP)
    )
    out[...] = (own[...] + total * scale).astype(BF)


def finish(arr, own):
    return pl.pallas_call(
        finish_kernel,
        out_shape=jax.ShapeDtypeStruct((MB, W), BF),
        in_specs=[vspec()] * 2,
        out_specs=vspec(),
        compiler_params=params(8),
        name="finish",
    )(arr, own)


def exchange(x, axis, size, first):
    groups = [[(i + first) % size for i in range(size)]]
    return lax.all_to_all(
        x, axis, split_axis=0, concat_axis=0, tiled=True, axis_index_groups=groups
    )


def per_device(
    candidates,
    actions,
    hist_keys,
    hist_values,
    w_query,
    w_gate,
    w_key,
    w_value,
    w_out,
    segment_list,
    segment_count,
    segment_length,
    new_count,
    batch_user,
):
    with jax.named_scope("gather"):
        message, own, info, mask = project(
            segment_list,
            segment_count,
            segment_length,
            new_count,
            batch_user,
            candidates,
            actions,
            w_query,
            w_key,
            w_value,
        )
        arrived = exchange(message, "z", NZ, FIRST_Z)
    with jax.named_scope("share"):
        mine = stage(info, own, hist_keys, hist_values)
        theirs = lax.ppermute(mine, "core", [(0, 1), (1, 0)])
        gate, base, residual = gate_and_base(candidates, w_gate, w_out)
        arrived, gate, base, residual = lax.optimization_barrier(
            (arrived, gate, base, residual)
        )
    with jax.named_scope("gather"):
        arrived = exchange(spread(arrived.reshape(ZROWS, W + DH)), "x", NX, FIRST_X)
    with jax.named_scope("attend"):
        part, fresh = attend(mask, arrived, mine, theirs)
    with jax.named_scope("return"):
        part = exchange(part, "x", NX, FIRST_X)
    with jax.named_scope("append"):
        fresh = lax.all_gather(fresh, "core", axis=0).reshape(XC, ZROWS, DH)
        new_keys, new_values = append(info, fresh, hist_keys, hist_values)
    with jax.named_scope("return"):
        part, new_keys, new_values = lax.optimization_barrier((part, new_keys, new_values))
        summed = exchange(fold(part), "z", NZ, FIRST_Z)
    with jax.named_scope("mix"):
        mixed = exchange(mix(summed, gate, base, w_out), "mp", MP, FIRST_Y)
        ranked = finish(mixed, residual)
    return (ranked, new_keys, new_values)


def solution(mesh):
    names = ("z", "x", "core", "mp")
    inner = Mesh(mesh.devices.reshape(NZ, NX, NC, MP), names)
    hist = ("z", "x", "core")
    in_specs = (
        P(hist, None),
        P(hist, None),
        P(hist, "mp"),
        P(hist, "mp"),
        P(None, "mp"),
        P(None, "mp"),
        P(None, "mp"),
        P(None, "mp"),
        P("mp", None),
        P(),
        P(),
        P(),
        P(),
        P(),
    )
    out_specs = (P(hist, "mp"), P(hist, "mp"), P(hist, "mp"))
    return jax.shard_map(
        per_device, mesh=inner, in_specs=in_specs, out_specs=out_specs, check_vma=False
    )
```

```python
import functools
import math

import jax
import jax.numpy as jnp
from jax import lax
from jax.experimental import pallas as pl
from jax.experimental.pallas import tpu as pltpu
from jax.sharding import Mesh
from jax.sharding import PartitionSpec as P

D = 1024
DH = 128
SEG = 512
NEW = 64
USERS = 4
NZ = 16
NX = 4
NC = 2
XC = NX * NC
ZX = NZ * NX
MP = 4
MB = 8
SEG_DEV = 2
W = D // MP
HEADS = W // DH
BATCHES = NZ * XC
QROWS = BATCHES * MB
HALF = ZX * MB
ZROWS = NZ * MB
FIRST_Z = 8
FIRST_X = 3
FIRST_Y = 3
STORED = SEG_DEV * SEG
OWN = 16
PATCH = NEW + 16
HEAD = SEG // 4
ACT = 2
SCALE = 1.0 / math.sqrt(DH)
LOG2E = 1.4426950408889634
BF = jnp.bfloat16
F32 = jnp.float32
MIB = 1024 * 1024


def vspec():
    return pl.BlockSpec(memory_space=pltpu.VMEM)


def sspec():
    return pl.BlockSpec(memory_space=pltpu.SMEM)


def aspec():
    return pl.BlockSpec(memory_space=pl.ANY)


def params(mib):
    return pltpu.CompilerParams(vmem_limit_bytes=mib * MIB)


def cost(flops, nbytes):
    return pl.CostEstimate(flops=flops, bytes_accessed=nbytes, transcendentals=0)


def place():
    core = lax.axis_index("core")
    return core, lax.axis_index("z") * XC + lax.axis_index("x") * NC + core


def project_kernel(*refs):
    small, big, outs = refs[:5], refs[5:10], refs[10:14]
    scalars, vectors, weights = refs[14:18], refs[18:20], refs[20:23]
    rows, block, marks, sems = refs[23:]
    msg, own, info, mask = outs
    cand, act = big[:2]
    heavy = [
        pltpu.make_async_copy(x, y, sems.at[i])
        for i, (x, y) in enumerate(zip(big[2:], weights))
    ]
    sources = small[:4] + (small[0], small[4])
    light = [
        pltpu.make_async_copy(x, y, sems.at[3 + i])
        for i, (x, y) in enumerate(zip(sources, scalars + vectors))
    ]
    for copy in heavy[:1] + light + heavy[1:]:
        copy.start()
    block[...] = jnp.zeros_like(block)
    marks[...] = jnp.zeros_like(marks)
    for copy in light:
        copy.wait()

    lists, counts, lengths, news = scalars
    core, device = place()
    ends = [lists[u, counts[u] - 1] for u in range(USERS)]
    for s in range(SEG_DEV):
        segment = device * SEG_DEV + s
        added = jnp.int32(0)
        user = jnp.int32(0)
        for u in range(USERS):
            hit = ends[u] == segment
            added = jnp.where(hit, news[u], added)
            user = jnp.where(hit, u, user)
        info[s, 0] = lengths[segment]
        info[s, 1] = added
        info[s, 2] = user

    act_user = device * ACT // NEW
    listed = vectors[0][...]
    listing = lax.broadcasted_iota(jnp.int32, listed.shape, 0).astype(F32)
    users = vectors[1][...]
    batch = users.astype(F32)
    for c in range(NC):
        near = device if c == 0 else device + 1 - 2 * core
        for s in range(SEG_DEV):
            hit = listed == near * SEG_DEV + s
            owner = jnp.sum(jnp.where(hit, listing, 0.0), axis=0, keepdims=True)
            owner = jnp.sum(owner, axis=1, keepdims=True)
            k = c * SEG_DEV + s
            marks[k : k + 1] = jnp.where(batch == owner, 1.0, 0.0)
    marks[4:5] = jnp.where(users == act_user, 1.0, 0.0)
    mask[...] = marks[...].astype(BF)

    q, k, v = weights
    heavy[0].wait()
    query = jnp.dot(cand[...], q[...], preferred_element_type=F32).astype(BF)
    heavy[1].wait()
    key = jnp.dot(act[...], k[...], preferred_element_type=F32)
    heavy[2].wait()
    value = jnp.dot(act[...], v[...], preferred_element_type=F32)
    block[0:2] = key
    block[2:4] = value
    for h in range(HEADS):
        rows[h * 4 : h * 4 + 4] = block[0:4, h * DH : (h + 1) * DH]
    fresh = rows[...].astype(BF)
    for i in range(NZ):
        msg[i, :, 0:W] = query
        msg[i, :, W : W + DH] = fresh
    valid = jnp.clip(news[act_user] - device * ACT % NEW, 0, ACT)
    row = lax.broadcasted_iota(jnp.int32, (ACT, W), 0)
    block[...] = jnp.zeros_like(block)
    block[OWN - ACT : OWN] = key
    own[0] = block[...].astype(BF)
    block[OWN - ACT : OWN] = jnp.where(row < valid, value, 0.0)
    own[1] = block[...].astype(BF)


def project(lists, counts, lengths, news, users, cand, act, wq, wk, wv):
    weight = pltpu.VMEM((D, W), BF)
    return pl.pallas_call(
        project_kernel,
        out_shape=(
            jax.ShapeDtypeStruct((NZ, MB, W + DH), BF),
            jax.ShapeDtypeStruct((2, OWN, W), BF),
            jax.ShapeDtypeStruct((SEG_DEV, 3), jnp.int32),
            jax.ShapeDtypeStruct((8, BATCHES), BF),
        ),
        in_specs=[aspec()] * 5 + [vspec()] * 2 + [aspec()] * 3,
        out_specs=(vspec(), vspec(), sspec(), vspec()),
        scratch_shapes=[
            pltpu.SMEM(lists.shape, jnp.int32),
            pltpu.SMEM(counts.shape, jnp.int32),
            pltpu.SMEM(lengths.shape, jnp.int32),
            pltpu.SMEM(news.shape, jnp.int32),
            pltpu.VMEM(lists.shape, jnp.int32),
            pltpu.VMEM((1, BATCHES), jnp.int32),
            weight,
            weight,
            weight,
            pltpu.VMEM((MB, DH), F32),
            pltpu.VMEM((OWN, W), F32),
            pltpu.VMEM((8, BATCHES), F32),
            pltpu.SemaphoreType.DMA((9,)),
        ],
        name="project",
    )(lists, counts, lengths, news, users.reshape(1, BATCHES), cand, act, wq, wk, wv)


def stage_kernel(info, own, keys, vals, out):
    rowpos = lax.broadcasted_iota(jnp.int32, (SEG, W), 0)
    for s in range(SEG_DEV):
        lo = s * SEG
        out[lo : lo + SEG] = keys[lo : lo + SEG]
        v = vals[lo : lo + SEG].astype(F32)
        lo += STORED
        out[lo : lo + SEG] = jnp.where(rowpos < info[s, 0], v, 0.0).astype(BF)
    row = lax.broadcasted_iota(jnp.int32, (OWN, W), 0)
    last = keys[SEG - OWN : SEG].astype(F32)
    last = jnp.where(row >= OWN - ACT, own[0].astype(F32), last)
    out[SEG - OWN : SEG] = last.astype(BF)
    out[STORED + SEG - OWN : STORED + SEG] = own[1]


def stage(info, own, keys, vals):
    return pl.pallas_call(
        stage_kernel,
        out_shape=jax.ShapeDtypeStruct((2 * STORED, W), BF),
        in_specs=[sspec()] + [vspec()] * 3,
        out_specs=vspec(),
        compiler_params=params(16),
        cost_estimate=cost(1_000_000, 2_200_000),
        name="stage",
    )(info, own, keys, vals)


def spread_kernel(arr, out):
    rows = arr[...]
    for t in range(NX):
        out[t] = rows


def spread(arr):
    return pl.pallas_call(
        spread_kernel,
        out_shape=jax.ShapeDtypeStruct((NX, ZROWS, W + DH), BF),
        in_specs=[vspec()],
        out_specs=vspec(),
        compiler_params=params(8),
        name="spread",
    )(arr)


def append_kernel(info, arr, keys, vals, new_keys, new_vals, patch, sems):
    pairs = ((keys, new_keys), (vals, new_vals))
    copies = []
    for s in range(SEG_DEV):
        rows = pl.ds(s * SEG, HEAD)
        for i, (old, new) in enumerate(pairs):
            copies.append(
                pltpu.make_async_copy(old.at[rows], new.at[rows], sems.at[s * 2 + i])
            )
            copies[-1].start()

    shape = (PATCH, XC * 4 * MB)
    j = lax.broadcasted_iota(jnp.int32, shape, 1)
    source = ((j // 32 + FIRST_X) % NX) * NC + j // 128
    step = ((j // 8) % 4) * 16 + source * 2 + j % 2
    kind = (j // 2) % 4
    for s in range(SEG_DEV):
        length = info[s, 0]
        begin = jnp.clip((length // 16) * 16, HEAD, SEG - PATCH)
        rows = pl.ds(pl.multiple_of(s * SEG + begin, 16), PATCH)
        inner = pl.ds(pl.multiple_of(begin - HEAD, 16), PATCH)
        tail = pl.ds(s * SEG + HEAD, SEG - HEAD)
        start = ((info[s, 2] * 4 + (NZ - FIRST_Z)) % NZ) * MB
        fresh = arr[:, pl.ds(pl.multiple_of(start, 4 * MB), 4 * MB), :]
        fresh = fresh.reshape(XC * 4 * MB, DH)
        match = lax.broadcasted_iota(jnp.int32, shape, 0) + (begin - length) == step
        rowpos = lax.broadcasted_iota(jnp.int32, (PATCH, DH), 0) + (begin - length)
        fill = (rowpos >= 0) & (rowpos < info[s, 1])
        for i, (old, new) in enumerate(pairs):
            slot = s * 2 + i
            patch[slot] = old[tail]
            for h in range(HEADS):
                cs = slice(h * DH, (h + 1) * DH)
                hot = (match & (kind == 2 * h + i)).astype(F32).astype(BF)
                placed = jnp.dot(hot, fresh, preferred_element_type=F32)
                kept = old[rows, cs].astype(F32)
                patch[slot, inner, cs] = jnp.where(fill, placed, kept).astype(BF)
            copies.append(
                pltpu.make_async_copy(patch.at[slot], new.at[tail], sems.at[4 + slot])
            )
            copies[-1].start()
    for copy in copies:
        copy.wait()


def append(info, arr, keys, vals):
    stored = jax.ShapeDtypeStruct((STORED, W), BF)
    return pl.pallas_call(
        append_kernel,
        out_shape=(stored,) * 2,
        in_specs=[sspec()] + [vspec()] * 3,
        out_specs=(aspec(),) * 2,
        scratch_shapes=[
            pltpu.VMEM((SEG_DEV * 2, SEG - HEAD, W), BF),
            pltpu.SemaphoreType.DMA((SEG_DEV * 4,)),
        ],
        compiler_params=params(16),
        cost_estimate=cost(150_000_000, 2_500_000),
        name="append",
    )(info, arr, keys, vals)


def attend_kernel(maskrow, arr, mine, other, part, fresh, theirs, total, sem):
    copy = pltpu.make_async_copy(other, theirs, sem)
    copy.start()
    fresh[...] = arr[:, :, W:]
    shape = (HALF, BATCHES)
    row = lax.broadcasted_iota(jnp.int32, shape, 0)
    lane = lax.broadcasted_iota(jnp.int32, shape, 1)
    step = (row % ZROWS) // MB
    column = (row // ZROWS + FIRST_X) % NX
    batch = ((step + FIRST_Z) % NZ) * XC + column * NC + lax.axis_index("core")
    hot = (lane == batch).astype(F32).astype(BF)
    use = lax.dot_general(
        hot, maskrow[...], (((1,), (1,)), ((), ())), preferred_element_type=F32
    )

    def weigh(logits):
        e = jnp.exp2(logits * (-SCALE * LOG2E))
        return (logits * SCALE) * pl.reciprocal(1.0 + e, approx=True)

    def score(a, b):
        return lax.dot_general(a, b, (((1,), (1,)), ((), ())), preferred_element_type=F32)

    lane = lax.broadcasted_iota(jnp.int32, (HALF, DH), 1)
    marks = []
    for u in range(NC * SEG_DEV):
        seg = jnp.broadcast_to(use[:, u : u + 1], (HALF, DH))
        edge = jnp.where(lane >= DH - ACT, use[:, 4:5], seg)
        marks.append((seg.astype(BF), edge.astype(BF)))

    def stored(c, src, h):
        cs = slice(h * DH, (h + 1) * DH)
        logits = score(q[:, cs], src[0:STORED, cs])
        parts = []
        for i in range(STORED // DH):
            s = i * DH // SEG
            last = s == 0 and (i + 1) * DH == SEG
            mark = marks[c * SEG_DEV + s][1 if last else 0]
            parts.append(weigh(logits[:, i * DH : (i + 1) * DH]).astype(BF) * mark)
        wt = jnp.concatenate(parts, axis=1)
        return jnp.dot(wt, src[STORED : 2 * STORED, cs], preferred_element_type=F32)

    q = arr[:, :, 0:W].reshape(HALF, W)
    for h in range(HEADS):
        total[:, h * DH : (h + 1) * DH] = stored(0, mine, h)
    copy.wait()
    for h in range(HEADS):
        cs = slice(h * DH, (h + 1) * DH)
        out = (total[:, cs] + stored(1, theirs, h)).astype(BF)
        for x in range(NX):
            part[x, :, cs] = out[x * ZROWS : (x + 1) * ZROWS]


def attend(maskrow, arr, mine, theirs):
    return pl.pallas_call(
        attend_kernel,
        out_shape=(
            jax.ShapeDtypeStruct((NX, ZROWS, W), BF),
            jax.ShapeDtypeStruct((NX, ZROWS, DH), BF),
        ),
        in_specs=[vspec()] * 3 + [aspec()],
        out_specs=(vspec(),) * 2,
        scratch_shapes=[
            pltpu.VMEM((2 * STORED, W), BF),
            pltpu.VMEM((HALF, W), F32),
            pltpu.SemaphoreType.DMA,
        ],
        compiler_params=params(32),
        name="attend",
    )(maskrow, arr, mine, theirs)


def fold_kernel(arr, out):
    out[...] = jnp.sum(arr[...].astype(F32), axis=0).astype(BF)


def fold(arr):
    return pl.pallas_call(
        fold_kernel,
        out_shape=jax.ShapeDtypeStruct((ZROWS, W), BF),
        in_specs=[vspec()],
        out_specs=vspec(),
        compiler_params=params(8),
        name="fold",
    )(arr)


def two_terms(x):
    hi = x.astype(BF)
    lo = (x - hi.astype(F32)).astype(BF)
    return hi, lo


def gate_kernel(cand, wg, wo, gate, base, own):
    first = pl.multiple_of(lax.axis_index("mp") * W, W)
    own[...] = cand[:, pl.ds(first, W)].astype(F32)
    v = jnp.dot(cand[...], wg[...], preferred_element_type=F32)
    g = v / (1.0 + jnp.exp(-v))
    gate[...] = g
    hi, lo = two_terms(g)
    base[...] = jnp.dot(hi, wo[...], preferred_element_type=F32) + jnp.dot(
        lo, wo[...], preferred_element_type=F32
    )


def gate_and_base(cand, wg, wo):
    return pl.pallas_call(
        gate_kernel,
        out_shape=(
            jax.ShapeDtypeStruct((MB, W), F32),
            jax.ShapeDtypeStruct((MB, D), F32),
            jax.ShapeDtypeStruct((MB, W), F32),
        ),
        in_specs=[vspec()] * 3,
        out_specs=(vspec(),) * 3,
        compiler_params=params(8),
        cost_estimate=cost(10_000_000_000, 40_000_000),
        name="gate",
    )(cand, wg, wo)


MSG = 2 * W + 128


def mix_kernel(arr, gate, base, wo, out):
    att = jnp.sum(arr[...].astype(F32).reshape(NZ, MB, W), axis=0)
    mean = jnp.sum(att, axis=1, keepdims=True) * (1.0 / W)
    d = att - mean
    sq = jnp.sum(d * d, axis=1, keepdims=True)
    hi, lo = two_terms(d * gate[...])
    a = jnp.dot(hi, wo[...], preferred_element_type=F32) + jnp.dot(
        lo, wo[...], preferred_element_type=F32
    )
    b = base[...]
    lane = lax.broadcasted_iota(jnp.int32, (MB, 128), 1)
    stats = jnp.where(lane == 0, mean, sq)
    for i in range(MP):
        cs = slice((i + FIRST_Y) % MP * W, ((i + FIRST_Y) % MP + 1) * W)
        out[i, :, 0:W] = a[:, cs]
        out[i, :, W : 2 * W] = b[:, cs]
        out[i, :, 2 * W : MSG] = stats


def mix(arr, gate, base, wo):
    return pl.pallas_call(
        mix_kernel,
        out_shape=jax.ShapeDtypeStruct((MP, MB, MSG), F32),
        in_specs=[vspec()] * 4,
        out_specs=vspec(),
        compiler_params=params(8),
        name="mix",
    )(arr, gate, base, wo)


def finish_kernel(arr, own, out):
    means = [arr[i, :, 2 * W : 2 * W + 1] for i in range(MP)]
    mean = sum(means) * (1.0 / MP)
    square = sum(arr[i, :, 2 * W + 1 : 2 * W + 2] for i in range(MP))
    square = square + W * sum((m - mean) * (m - mean) for m in means)
    scale = lax.rsqrt(square * (1.0 / D) + 1e-05)
    total = sum(
        arr[i, :, 0:W] + (means[i] - mean) * arr[i, :, W : 2 * W] for i in range(MP)
    )
    out[...] = (own[...] + total * scale).astype(BF)


def finish(arr, own):
    return pl.pallas_call(
        finish_kernel,
        out_shape=jax.ShapeDtypeStruct((MB, W), BF),
        in_specs=[vspec()] * 2,
        out_specs=vspec(),
        compiler_params=params(8),
        name="finish",
    )(arr, own)


def exchange(x, axis, size, first):
    groups = [[(i + first) % size for i in range(size)]]
    return lax.all_to_all(
        x, axis, split_axis=0, concat_axis=0, tiled=True, axis_index_groups=groups
    )


def per_device(
    candidates,
    actions,
    hist_keys,
    hist_values,
    w_query,
    w_gate,
    w_key,
    w_value,
    w_out,
    segment_list,
    segment_count,
    segment_length,
    new_count,
    batch_user,
):
    with jax.named_scope("gather"):
        message, own, info, mask = project(
            segment_list,
            segment_count,
            segment_length,
            new_count,
            batch_user,
            candidates,
            actions,
            w_query,
            w_key,
            w_value,
        )
        arrived = exchange(message, "z", NZ, FIRST_Z)
    with jax.named_scope("share"):
        mine = stage(info, own, hist_keys, hist_values)
        theirs = lax.ppermute(mine, "core", [(0, 1), (1, 0)])
        gate, base, residual = gate_and_base(candidates, w_gate, w_out)
        arrived, gate, base, residual = lax.optimization_barrier(
            (arrived, gate, base, residual)
        )
    with jax.named_scope("gather"):
        arrived = exchange(spread(arrived.reshape(ZROWS, W + DH)), "x", NX, FIRST_X)
    with jax.named_scope("attend"):
        part, fresh = attend(mask, arrived, mine, theirs)
    with jax.named_scope("return"):
        part = exchange(part, "x", NX, FIRST_X)
    with jax.named_scope("append"):
        fresh = lax.all_gather(fresh, "core", axis=0).reshape(XC, ZROWS, DH)
        new_keys, new_values = append(info, fresh, hist_keys, hist_values)
    with jax.named_scope("return"):
        part, new_keys, new_values = lax.optimization_barrier((part, new_keys, new_values))
        summed = exchange(fold(part), "z", NZ, FIRST_Z)
    with jax.named_scope("mix"):
        mixed = exchange(mix(summed, gate, base, w_out), "mp", MP, FIRST_Y)
        ranked = finish(mixed, residual)
    return (ranked, new_keys, new_values)


def solution(mesh):
    names = ("z", "x", "core", "mp")
    inner = Mesh(mesh.devices.reshape(NZ, NX, NC, MP), names)
    hist = ("z", "x", "core")
    in_specs = (
        P(hist, None),
        P(hist, None),
        P(hist, "mp"),
        P(hist, "mp"),
        P(None, "mp"),
        P(None, "mp"),
        P(None, "mp"),
        P(None, "mp"),
        P("mp", None),
        P(),
        P(),
        P(),
        P(),
        P(),
    )
    out_specs = (P(hist, "mp"), P(hist, "mp"), P(hist, "mp"))
    return jax.shard_map(
        per_device, mesh=inner, in_specs=in_specs, out_specs=out_specs, check_vma=False
    )
```
